512 devices in a mesh: gy: 16 (over y, core), gx: 32 (over z, x).
Axes of the slice: x: 4, y: 8, z: 8, core: 2. Of those that a mesh axis runs over, the one named last changes fastest.
Arguments:
- pressure: float32 [512, 256, 128], P('gx', 'gy'), may hold values from -0.03 to 0.03
- source: float32 [512, 256, 128], P('gx', 'gy'), may hold values from -0.2 to 0.2
- porosity: bfloat16 [512, 256, 128], P('gx', 'gy'), may hold values from 0.079589844 to 0.34960938
- permeability: bfloat16 [512, 256, 128], P('gx', 'gy'), may hold values from 0.25 to 4
- speed: bfloat16 [512, 256, 128], P('gx', 'gy'), may hold values from 0.099609375 to 3
Outputs:
- updated: float32 [512, 256, 128], P('gx', 'gy')
The draws below stay inside these ranges and needn't reach their ends.
All inputs are finite; a program needn't handle non-finite values.
Results may differ from the reference program's by a relative error of at most 0.0003.
Values sent between devices are 32-bit elements; how exact they have to be, the bound alone decides.
No kernel may reach another device: no remote copies, remote signals or barrier semaphores. Data moves between devices by JAX's collectives and lax.ppermute only.
A program may use at most 64 MiB of HBM per device.

```python
import math
import jax
import jax.numpy as jnp
from jax import lax

NX = 512
NY = 256
NZ = 128


def draw_source(key, part):
    values = jnp.clip(0.025 * jax.random.normal(key, (NX, NY, NZ), jnp.float32), -0.2, 0.2)
    return values


def level_of(own_key, extent, cuts, low, largest):
    level = 1.0
    for position, shards_of in cuts:
        heights = jax.random.uniform(jax.random.fold_in(jax.random.fold_in(own_key, 6), position), (shards_of,), jnp.float32, low / len(cuts), largest / len(cuts))
        level = level * jnp.repeat(jnp.exp(heights), extent[position] // shards_of).reshape((-1,) + (1,) * (len(extent) - 1 - position))
    return level


def bell_draw(own_key, dims, spread, most, shards=(), dtype=jnp.bfloat16):
    drawn = spread * jax.random.normal(own_key, dims, jnp.float32)
    if shards:
        drawn = drawn * level_of(own_key, dims, shards, -0.22, 0.18)
    return jnp.clip(drawn, -most, most).astype(dtype)


def setup_inputs(seed: int = 0) -> dict:
    key_list = jax.random.split(jax.random.key(seed), 6)
    pressure = bell_draw(key_list[0], (NX, NY, NZ), 0.005, 0.03, ((0, 32), (1, 16)), jnp.float32)
    source = draw_source(jax.random.fold_in(key_list[5], 71), 0)
    porosity = jnp.clip(jnp.exp(math.log(0.34960938) - 1.47992997 * jax.random.uniform(key_list[2], (NX, NY, NZ), jnp.float32) ** level_of(key_list[2], (NX, NY, NZ), ((0, 32), (1, 16)), -0.2, 0.2)), 0.079589844, 0.34960938).astype(jnp.bfloat16)
    permeability = jnp.clip(jnp.exp(math.log(4.0) - 2.7725887 * jax.random.uniform(key_list[3], (NX, NY, NZ), jnp.float32) ** level_of(key_list[3], (NX, NY, NZ), ((0, 32), (1, 16)), -0.2, 0.2)), 0.25, 4.0).astype(jnp.bfloat16)
    speed = jnp.clip(jnp.exp(math.log(3.0) - 3.4051113 * jax.random.uniform(key_list[4], (NX, NY, NZ), jnp.float32) ** level_of(key_list[4], (NX, NY, NZ), ((0, 32), (1, 16)), -0.2, 0.2)), 0.099609375, 3.0).astype(jnp.bfloat16)
    return {"pressure": pressure, "source": source, "porosity": porosity, "permeability": permeability, "speed": speed}


forch_coeff = 0.55
time_step = 500.0

def harmonic(first, second):
    return 2.0 * first * second / (first + second)

def mobility(permeability, speed):
    perm_cells = permeability.astype(jnp.float32)
    return perm_cells / (1.0 + forch_coeff * jnp.sqrt(perm_cells) * speed.astype(jnp.float32))

def thomas(lower_diag, main_diag, upper_diag, right_side):

    def forward(carry, row):
        ratio_prev, value_prev = carry
        low_row, main_row, up_row, rhs_row = row
        divisor = main_row - low_row * ratio_prev
        ratio = up_row / divisor
        value = (rhs_row - low_row * value_prev) / divisor
        return ((ratio, value), (ratio, value))
    zeros_row = jnp.zeros_like(right_side[0])
    _, (ratios, values) = lax.scan(forward, (zeros_row, zeros_row), (lower_diag, main_diag, upper_diag, right_side))

    def backward(after, row):
        ratio, value = row
        result = value - ratio * after
        return (result, result)
    _, solved = lax.scan(backward, zeros_row, (ratios, values), reverse=True)
    return solved

def swap_axes(values):
    return jnp.transpose(values, (1, 0, 2))

def reference(pressure, source, porosity, permeability, speed):
    mobility_field = mobility(permeability, speed)
    padded_mob = jnp.pad(mobility_field, 1)
    padded_p = jnp.pad(pressure, 1)
    face_xp = harmonic(mobility_field, padded_mob[2:, 1:-1, 1:-1])
    face_xm = harmonic(mobility_field, padded_mob[:-2, 1:-1, 1:-1])
    face_yp = harmonic(mobility_field, padded_mob[1:-1, 2:, 1:-1])
    face_ym = harmonic(mobility_field, padded_mob[1:-1, :-2, 1:-1])
    face_zp = harmonic(mobility_field, padded_mob[1:-1, 1:-1, 2:])
    face_zm = harmonic(mobility_field, padded_mob[1:-1, 1:-1, :-2])
    laplacian = face_xp * (padded_p[2:, 1:-1, 1:-1] - pressure) + face_xm * (padded_p[:-2, 1:-1, 1:-1] - pressure)
    laplacian = laplacian + face_yp * (padded_p[1:-1, 2:, 1:-1] - pressure) + face_ym * (padded_p[1:-1, :-2, 1:-1] - pressure)
    laplacian = laplacian + face_zp * (padded_p[1:-1, 1:-1, 2:] - pressure) + face_zm * (padded_p[1:-1, 1:-1, :-2] - pressure)
    residual_field = laplacian - source
    ratio_field = porosity.astype(jnp.float32) / time_step
    along_x = thomas(-face_xm, ratio_field + face_xm + face_xp, -face_xp, residual_field)
    correction = thomas(swap_axes(-face_ym), swap_axes(ratio_field + face_ym + face_yp), swap_axes(-face_yp), swap_axes(ratio_field * along_x))
    return pressure + swap_axes(correction)
```

```python
import jax
import jax.numpy as jnp
from jax import lax
from jax.experimental import pallas as pl
from jax.experimental.pallas import tpu as pltpu
from jax.sharding import PartitionSpec as P

FORCH = 0.55
STEP = 500.0
NEAR_X = 4
NEAR_Y = 2
F32 = jnp.float32


def join(left, right):
    la, lb, lc, lg, lh = left
    ra, rb, rc, rg, rh = right
    inv = 1.0 / (lc + ra)
    left_share = lb * inv
    right_share = rb * inv
    gap = lh - rg
    merged = (
        la - lb * left_share,
        lb * right_share,
        rc - rb * right_share,
        lg - left_share * gap,
        rh + right_share * gap,
    )
    return merged, (inv * gap, left_share, right_share)


def join_all(pieces):
    if len(pieces) == 1:
        return pieces[0], None
    half = len(pieces) // 2
    left, left_tree = join_all(pieces[:half])
    right, right_tree = join_all(pieces[half:])
    merged, face = join(left, right)
    return merged, (face, left_tree, right_tree)


def face_fluxes(tree, low, high):
    if tree is None:
        return [low, high]
    face, left_tree, right_tree = tree
    flux = face[0]
    if low is not None:
        flux = flux + face[1] * low
    if high is not None:
        flux = flux + face[2] * high
    return face_fluxes(left_tree, low, flux) + face_fluxes(right_tree, flux, high)[1:]


def tree_shape(count):
    if count == 1:
        return None
    return (count, tree_shape(count // 2), tree_shape(count // 2))


def tree_values(tree):
    if tree is None:
        return []
    return list(tree[0]) + tree_values(tree[1]) + tree_values(tree[2])


def tree_of(shape, values):
    if shape is None:
        return None
    face = tuple(values.pop(0) for _ in range(3))
    left = tree_of(shape[1], values)
    return (face, left, tree_of(shape[2], values))


def plane(ref, i, rows):
    return ref[i * rows : (i + 1) * rows, :]


def eliminate(ratio, half, count):
    gaps = [half[i] + half[i + 1] for i in range(count - 1)]
    up = []
    total = ratio[0]
    for i in range(count - 1):
        carry = 1.0 / (1.0 + total * gaps[i])
        up.append(carry)
        total = ratio[i + 1] + total * carry
    last_inv = 1.0 / total
    down = [None] * (count - 1)
    total = ratio[count - 1]
    for i in range(count - 2, -1, -1):
        carry = 1.0 / (1.0 + total * gaps[i])
        down[i] = carry
        total = ratio[i] + total * carry
    first_inv = 1.0 / total
    across = last_inv
    for i in range(count - 2, -1, -1):
        across = across * up[i]
    ends = [first_inv + half[0], across, last_inv + half[count - 1], first_inv, last_inv]
    return gaps, up, down, ends


def offsets(right, up, down, first_inv, last_inv, count):
    rising = right[0]
    for i in range(count - 1):
        rising = right[i + 1] + up[i] * rising
    falling = right[count - 1]
    for i in range(count - 2, -1, -1):
        falling = right[i] + down[i] * falling
    return falling * first_inv, rising * last_inv


def substitute(right, gaps, up, last_inv, low, high, count):
    sums = [right[0] + low]
    for i in range(count - 1):
        sums.append(right[i + 1] + up[i] * sums[i])
    values = [None] * count
    values[count - 1] = (sums[count - 1] - high) * last_inv
    for i in range(count - 2, -1, -1):
        values[i] = up[i] * (values[i + 1] + gaps[i] * sums[i])
    return values


def local_step(sizes, sizes_mesh, pressure, source, porosity, permeability, speed):
    nx, ny, nz = sizes
    count_gx, count_gy = sizes_mesh
    far_x = count_gx // NEAR_X
    far_y = count_gy // NEAR_Y
    near_x_groups = [[z * NEAR_X + x for x in range(NEAR_X)] for z in range(far_x)]
    far_x_groups = [[z * NEAR_X + x for z in range(far_x)] for x in range(NEAR_X)]
    far_y_groups = [[y * NEAR_Y + c for y in range(far_y)] for c in range(NEAR_Y)]
    cells = nx * ny
    pressure = pressure.reshape(cells, nz)
    source = source.reshape(cells, nz)
    porosity = porosity.reshape(cells, nz)
    permeability = permeability.reshape(cells, nz)
    speed = speed.reshape(cells, nz)

    def call(body, shapes, scratch, *args, name):
        return pl.pallas_call(
            body,
            out_shape=[jax.ShapeDtypeStruct(s, F32) for s in shapes],
            in_specs=[pl.BlockSpec(memory_space=pltpu.VMEM)] * len(args),
            out_specs=[pl.BlockSpec(memory_space=pltpu.VMEM)] * len(shapes),
            scratch_shapes=[pltpu.VMEM(s, F32) for s in scratch],
            compiler_params=pltpu.CompilerParams(vmem_limit_bytes=32 * 1024 * 1024),
            name=name,
        )(*args)

    def rows_y(ref, j):
        return ref[pl.ds(j, nx, stride=ny), :]

    def halves_body(perm_ref, speed_ref, p_ref, half_ref, near_ref, far_ref):
        for i in range(nx):
            root = lax.rsqrt(plane(perm_ref, i, ny).astype(F32))
            half_ref[i * ny : (i + 1) * ny, :] = (0.5 * root) * (
                root + FORCH * plane(speed_ref, i, ny).astype(F32)
            )
        even = lax.rem(lax.axis_index("gy"), 2) == 0
        for k, ref in enumerate((half_ref, p_ref)):
            low = rows_y(ref, 0)
            high = rows_y(ref, ny - 1)
            near_ref[k] = jnp.where(even, high, low)
            far_ref[k] = jnp.where(even, low, high)

    half, near_send, far_send = call(
        halves_body, [(cells, nz), (2, nx, nz), (2, nx, nz)], [], permeability, speed, pressure,
        name="halves",
    )
    far_pairs = []
    for i in range(1, count_gy - 1, 2):
        far_pairs += [(i, i + 1), (i + 1, i)]
    far_got = lax.ppermute(far_send, "gy", far_pairs)
    near_got = lax.ppermute(near_send, "gy", [(i, i ^ 1) for i in range(count_gy)])

    def inner_body(
        p_ref, source_ref, por_ref, half_ref,
        right_ref, ratio_ref, xup_ref, xdown_ref, xends_ref, yup_ref, ydown_ref, yends_ref,
    ):
        lane = lax.broadcasted_iota(jnp.int32, (ny, nz), 1)
        row = lax.broadcasted_iota(jnp.int32, (ny, nz), 0)
        for i in range(nx):
            p = plane(p_ref, i, ny)
            h = plane(half_ref, i, ny)
            ratio = plane(por_ref, i, ny).astype(F32) * (1.0 / STEP)
            ratio_ref[i * ny : (i + 1) * ny, :] = ratio
            flux_z = (pltpu.roll(p, nz - 1, 1) - p) / (pltpu.roll(h, nz - 1, 1) + h)
            flux_z = jnp.where(lane == nz - 1, 0.0, flux_z)
            flux_y = (pltpu.roll(p, ny - 1, 0) - p) / (pltpu.roll(h, ny - 1, 0) + h)
            flux_y = jnp.where(row == ny - 1, 0.0, flux_y)
            lap = (flux_z - pltpu.roll(flux_z, 1, 1)) + (flux_y - pltpu.roll(flux_y, 1, 0))
            right_ref[i * ny : (i + 1) * ny, :] = (lap - plane(source_ref, i, ny)) + ratio * p
        ratios = [plane(ratio_ref, i, ny) for i in range(nx)]
        halves = [plane(half_ref, i, ny) for i in range(nx)]
        _, up, down, ends = eliminate(ratios, halves, nx)
        for i in range(nx - 1):
            xup_ref[i] = up[i]
            xdown_ref[i] = down[i]
        for k in range(5):
            xends_ref[k] = ends[k]
        ratios = [rows_y(ratio_ref, j) for j in range(ny)]
        halves = [rows_y(half_ref, j) for j in range(ny)]
        _, up, down, ends = eliminate(ratios, halves, ny)
        for j in range(ny - 1):
            yup_ref[j] = up[j]
            ydown_ref[j] = down[j]
        for k in range(5):
            yends_ref[k] = ends[k]

    right0, ratio, xup, xdown, xends, yup, ydown, yends = call(
        inner_body,
        [
            (cells, nz), (cells, nz), (nx - 1, ny, nz), (nx - 1, ny, nz), (5, ny, nz),
            (ny - 1, nx, nz), (ny - 1, nx, nz), (5, nx, nz),
        ],
        [], pressure, source, porosity, half, name="inner",
    )

    def edges_body(
        right0_ref, p_ref, half_ref, near_ref, far_ref, xup_ref, xdown_ref, xends_ref, right_ref, send_ref
    ):
        place = lax.axis_index("gy")
        even = lax.rem(place, 2) == 0
        right_ref[...] = right0_ref[...]
        for j, is_end, low in ((0, place == 0, True), (ny - 1, place == count_gy - 1, False)):
            first, second = (far_ref, near_ref) if low else (near_ref, far_ref)
            other_h = jnp.where(even, first[0], second[0])
            other_p = jnp.where(even, first[1], second[1])
            flux = (other_p - rows_y(p_ref, j)) / (other_h + rows_y(half_ref, j))
            flux = jnp.where(is_end, 0.0, flux)
            right_ref[pl.ds(j, nx, stride=ny), :] = rows_y(right_ref, j) + flux
        right = [plane(right_ref, i, ny) for i in range(nx)]
        up = [xup_ref[i] for i in range(nx - 1)]
        down = [xdown_ref[i] for i in range(nx - 1)]
        first, last = offsets(right, up, down, xends_ref[3], xends_ref[4], nx)
        for k, value in enumerate((xends_ref[0], xends_ref[1], xends_ref[2], first, last)):
            for target in range(NEAR_X):
                send_ref[target, k] = value

    right, near_x = call(
        edges_body, [(cells, nz), (NEAR_X, 5, ny, nz)], [],
        right0, pressure, half, near_got, far_got, xup, xdown, xends, name="edges",
    )
    near_x = lax.all_to_all(near_x, "gx", 0, 0, axis_index_groups=near_x_groups)

    def ring_body(got_ref, send_ref, tree_ref):
        pieces = [tuple(got_ref[n, k] for k in range(5)) for n in range(NEAR_X)]
        merged, tree = join_all(pieces)
        for k in range(5):
            for target in range(far_x):
                send_ref[target, k] = merged[k]
        for k, value in enumerate(tree_values(tree)):
            tree_ref[k] = value

    far_x_send, x_tree = call(
        ring_body, [(far_x, 5, ny, nz), (3 * (NEAR_X - 1), ny, nz)], [], near_x, name="x_ring"
    )
    far_x_got = lax.all_to_all(far_x_send, "gx", 0, 0, axis_index_groups=far_x_groups)

    def along_x_body(
        got_ref, tree_ref, right_ref, half_ref, ratio_ref, p_ref, xup_ref, xends_ref,
        yup_ref, ydown_ref, yends_ref,
        send_ref, yright_ref, far_faces, near_faces, solved_ref,
    ):
        place = lax.axis_index("gx")
        far = place // NEAR_X
        near = lax.rem(place, NEAR_X)
        pieces = [tuple(got_ref[n, k] for k in range(5)) for n in range(far_x)]
        _, tree = join_all(pieces)
        fluxes = face_fluxes(tree, None, None)
        zero = jnp.zeros((ny, nz), F32)
        for k, value in enumerate(fluxes):
            far_faces[k] = zero if value is None else value
        low = far_faces[far]
        high = far_faces[far + 1]
        tree = tree_of(tree_shape(NEAR_X), [tree_ref[k] for k in range(3 * (NEAR_X - 1))])
        for k, value in enumerate(face_fluxes(tree, low, high)):
            near_faces[k] = value
        low = near_faces[near]
        high = near_faces[near + 1]
        gaps = [plane(half_ref, i, ny) + plane(half_ref, i + 1, ny) for i in range(nx - 1)]
        up = [xup_ref[i] for i in range(nx - 1)]
        right = [plane(right_ref, i, ny) for i in range(nx)]
        values = substitute(right, gaps, up, xends_ref[4], low, high, nx)
        for i in range(nx):
            solved_ref[i * ny : (i + 1) * ny, :] = plane(ratio_ref, i, ny) * (values[i] - plane(p_ref, i, ny))
        yright = [rows_y(solved_ref, j) for j in range(ny)]
        for j in range(ny):
            yright_ref[j] = yright[j]
        up = [yup_ref[j] for j in range(ny - 1)]
        down = [ydown_ref[j] for j in range(ny - 1)]
        first, last = offsets(yright, up, down, yends_ref[3], yends_ref[4], ny)
        for k, value in enumerate((yends_ref[0], yends_ref[1], yends_ref[2], first, last)):
            send_ref[k] = value

    pair_send, yright = call(
        along_x_body,
        [(5, nx, nz), (ny, nx, nz)],
        [(far_x + 1, ny, nz), (NEAR_X + 1, ny, nz), (cells, nz)],
        far_x_got, x_tree, right, half, ratio, pressure, xup, xends, yup, ydown, yends,
        name="along_x",
    )
    pair_got = lax.ppermute(pair_send, "gy", [(i, i ^ 1) for i in range(count_gy)])

    def pair_body(own_ref, got_ref, send_ref, tree_ref):
        even = lax.rem(lax.axis_index("gy"), 2) == 0
        left = tuple(jnp.where(even, own_ref[k], got_ref[k]) for k in range(5))
        right = tuple(jnp.where(even, got_ref[k], own_ref[k]) for k in range(5))
        merged, face = join(left, right)
        for k in range(5):
            for target in range(far_y):
                send_ref[target, k] = merged[k]
        for k in range(3):
            tree_ref[k] = face[k]

    far_y_send, y_tree = call(
        pair_body, [(far_y, 5, nx, nz), (3, nx, nz)], [], pair_send, pair_got, name="y_pair"
    )
    far_y_got = lax.all_to_all(far_y_send, "gy", 0, 0, axis_index_groups=far_y_groups)

    def updated_body(
        got_ref, tree_ref, yright_ref, half_ref, p_ref, yup_ref, yends_ref, out_ref, far_faces, near_faces
    ):
        place = lax.axis_index("gy")
        far = place // NEAR_Y
        near = lax.rem(place, NEAR_Y)
        pieces = [tuple(got_ref[n, k] for k in range(5)) for n in range(far_y)]
        _, tree = join_all(pieces)
        zero = jnp.zeros((nx, nz), F32)
        for k, value in enumerate(face_fluxes(tree, None, None)):
            far_faces[k] = zero if value is None else value
        low = far_faces[far]
        high = far_faces[far + 1]
        tree = tree_of(tree_shape(NEAR_Y), [tree_ref[k] for k in range(3)])
        for k, value in enumerate(face_fluxes(tree, low, high)):
            near_faces[k] = value
        low = near_faces[near]
        high = near_faces[near + 1]
        halves = [rows_y(half_ref, j) for j in range(ny)]
        gaps = [halves[j] + halves[j + 1] for j in range(ny - 1)]
        up = [yup_ref[j] for j in range(ny - 1)]
        right = [yright_ref[j] for j in range(ny)]
        values = substitute(right, gaps, up, yends_ref[4], low, high, ny)
        for j in range(ny):
            out_ref[pl.ds(j, nx, stride=ny), :] = rows_y(p_ref, j) + values[j]

    (updated,) = call(
        updated_body,
        [(cells, nz)],
        [(far_y + 1, nx, nz), (NEAR_Y + 1, nx, nz)],
        far_y_got, y_tree, yright, half, pressure, yup, yends,
        name="updated",
    )
    return updated.reshape(nx, ny, nz)


def solution(mesh):
    spec = P("gx", "gy", None)
    sizes_mesh = (mesh.shape["gx"], mesh.shape["gy"])

    def local(pressure, source, porosity, permeability, speed):
        return local_step(
            pressure.shape, sizes_mesh, pressure, source, porosity, permeability, speed
        )

    return jax.shard_map(
        local, mesh=mesh, in_specs=(spec,) * 5, out_specs=spec, check_vma=False
    )
```

```python
import jax
import jax.numpy as jnp
from jax import lax
from jax.experimental import pallas as pl
from jax.experimental.pallas import tpu as pltpu
from jax.sharding import PartitionSpec as P

FORCH = 0.55
STEP = 500.0
NEAR_X = 4
NEAR_Y = 2
F32 = jnp.float32


def join(left, right):
    la, lb, lc, lg, lh = left
    ra, rb, rc, rg, rh = right
    inv = 1.0 / (lc + ra)
    left_share = lb * inv
    right_share = rb * inv
    gap = lh - rg
    merged = (
        la - lb * left_share,
        lb * right_share,
        rc - rb * right_share,
        lg - left_share * gap,
        rh + right_share * gap,
    )
    return merged, (inv * gap, left_share, right_share)


def join_all(pieces):
    if len(pieces) == 1:
        return pieces[0], None
    half = len(pieces) // 2
    left, left_tree = join_all(pieces[:half])
    right, right_tree = join_all(pieces[half:])
    merged, face = join(left, right)
    return merged, (face, left_tree, right_tree)


def face_fluxes(tree, low, high):
    if tree is None:
        return [low, high]
    face, left_tree, right_tree = tree
    flux = face[0]
    if low is not None:
        flux = flux + face[1] * low
    if high is not None:
        flux = flux + face[2] * high
    return face_fluxes(left_tree, low, flux) + face_fluxes(right_tree, flux, high)[1:]


def tree_shape(count):
    if count == 1:
        return None
    return (count, tree_shape(count // 2), tree_shape(count // 2))


def tree_values(tree):
    if tree is None:
        return []
    return list(tree[0]) + tree_values(tree[1]) + tree_values(tree[2])


def tree_of(shape, values):
    if shape is None:
        return None
    face = tuple(values.pop(0) for _ in range(3))
    left = tree_of(shape[1], values)
    return (face, left, tree_of(shape[2], values))


def plane(ref, i, rows):
    return ref[i * rows : (i + 1) * rows, :]


def eliminate(ratio, half, count):
    gaps = [half[i] + half[i + 1] for i in range(count - 1)]
    up = []
    total = ratio[0]
    for i in range(count - 1):
        carry = 1.0 / (1.0 + total * gaps[i])
        up.append(carry)
        total = ratio[i + 1] + total * carry
    last_inv = 1.0 / total
    down = [None] * (count - 1)
    total = ratio[count - 1]
    for i in range(count - 2, -1, -1):
        carry = 1.0 / (1.0 + total * gaps[i])
        down[i] = carry
        total = ratio[i] + total * carry
    first_inv = 1.0 / total
    across = last_inv
    for i in range(count - 2, -1, -1):
        across = across * up[i]
    ends = [first_inv + half[0], across, last_inv + half[count - 1], first_inv, last_inv]
    return gaps, up, down, ends


def offsets(right, up, down, first_inv, last_inv, count):
    rising = right[0]
    for i in range(count - 1):
        rising = right[i + 1] + up[i] * rising
    falling = right[count - 1]
    for i in range(count - 2, -1, -1):
        falling = right[i] + down[i] * falling
    return falling * first_inv, rising * last_inv


def substitute(right, gaps, up, last_inv, low, high, count):
    sums = [right[0] + low]
    for i in range(count - 1):
        sums.append(right[i + 1] + up[i] * sums[i])
    values = [None] * count
    values[count - 1] = (sums[count - 1] - high) * last_inv
    for i in range(count - 2, -1, -1):
        values[i] = up[i] * (values[i + 1] + gaps[i] * sums[i])
    return values


def local_step(sizes, sizes_mesh, pressure, source, porosity, permeability, speed):
    nx, ny, nz = sizes
    count_gx, count_gy = sizes_mesh
    far_x = count_gx // NEAR_X
    far_y = count_gy // NEAR_Y
    near_x_groups = [[z * NEAR_X + x for x in range(NEAR_X)] for z in range(far_x)]
    far_x_groups = [[z * NEAR_X + x for z in range(far_x)] for x in range(NEAR_X)]
    far_y_groups = [[y * NEAR_Y + c for y in range(far_y)] for c in range(NEAR_Y)]
    cells = nx * ny
    pressure = pressure.reshape(cells, nz)
    source = source.reshape(cells, nz)
    porosity = porosity.reshape(cells, nz)
    permeability = permeability.reshape(cells, nz)
    speed = speed.reshape(cells, nz)

    def call(body, shapes, scratch, *args, name):
        return pl.pallas_call(
            body,
            out_shape=[jax.ShapeDtypeStruct(s, F32) for s in shapes],
            in_specs=[pl.BlockSpec(memory_space=pltpu.VMEM)] * len(args),
            out_specs=[pl.BlockSpec(memory_space=pltpu.VMEM)] * len(shapes),
            scratch_shapes=[pltpu.VMEM(s, F32) for s in scratch],
            compiler_params=pltpu.CompilerParams(vmem_limit_bytes=32 * 1024 * 1024),
            name=name,
        )(*args)

    def rows_y(ref, j):
        return ref[pl.ds(j, nx, stride=ny), :]

    def halves_body(
        p_hbm, source_hbm, por_hbm, perm_hbm, speed_hbm,
        half_ref, near_ref, far_ref, p_ref, source_ref, por_ref, perm_ref, speed_ref, sems,
    ):
        pairs = (
            (perm_hbm, perm_ref), (speed_hbm, speed_ref), (p_hbm, p_ref),
            (source_hbm, source_ref), (por_hbm, por_ref),
        )
        copies = [pltpu.make_async_copy(a, b, sems.at[n]) for n, (a, b) in enumerate(pairs)]
        for copy in copies:
            copy.start()
        for copy in copies[:3]:
            copy.wait()
        for i in range(nx):
            root = lax.rsqrt(plane(perm_ref, i, ny).astype(F32))
            half_ref[i * ny : (i + 1) * ny, :] = (0.5 * root) * (
                root + FORCH * plane(speed_ref, i, ny).astype(F32)
            )
        even = lax.rem(lax.axis_index("gy"), 2) == 0
        for k, ref in enumerate((half_ref, p_ref)):
            low = rows_y(ref, 0)
            high = rows_y(ref, ny - 1)
            near_ref[k] = jnp.where(even, high, low)
            far_ref[k] = jnp.where(even, low, high)
        for copy in copies[3:]:
            copy.wait()

    vmem = pl.BlockSpec(memory_space=pltpu.VMEM)
    half, near_send, far_send, pressure, source, porosity = pl.pallas_call(
        halves_body,
        out_shape=[
            jax.ShapeDtypeStruct((cells, nz), F32),
            jax.ShapeDtypeStruct((2, nx, nz), F32),
            jax.ShapeDtypeStruct((2, nx, nz), F32),
            jax.ShapeDtypeStruct((cells, nz), F32),
            jax.ShapeDtypeStruct((cells, nz), F32),
            jax.ShapeDtypeStruct((cells, nz), porosity.dtype),
        ],
        in_specs=[pl.BlockSpec(memory_space=pltpu.HBM)] * 5,
        out_specs=[vmem] * 6,
        scratch_shapes=[
            pltpu.VMEM((cells, nz), permeability.dtype),
            pltpu.VMEM((cells, nz), speed.dtype),
            pltpu.SemaphoreType.DMA((5,)),
        ],
        compiler_params=pltpu.CompilerParams(vmem_limit_bytes=16 * 1024 * 1024),
        name="halves",
    )(*(pltpu.with_memory_space_constraint(a, pltpu.HBM) for a in (pressure, source, porosity, permeability, speed)))
    far_pairs = []
    for i in range(1, count_gy - 1, 2):
        far_pairs += [(i, i + 1), (i + 1, i)]
    far_got = lax.ppermute(far_send, "gy", far_pairs)
    near_got = lax.ppermute(near_send, "gy", [(i, i ^ 1) for i in range(count_gy)])

    def inner_body(
        p_ref, source_ref, por_ref, half_ref,
        right_ref, ratio_ref, xup_ref, xdown_ref, xends_ref, yup_ref, ydown_ref, yends_ref,
    ):
        lane = lax.broadcasted_iota(jnp.int32, (ny, nz), 1)
        row = lax.broadcasted_iota(jnp.int32, (ny, nz), 0)
        for i in range(nx):
            p = plane(p_ref, i, ny)
            h = plane(half_ref, i, ny)
            ratio = plane(por_ref, i, ny).astype(F32) * (1.0 / STEP)
            ratio_ref[i * ny : (i + 1) * ny, :] = ratio
            flux_z = (pltpu.roll(p, nz - 1, 1) - p) / (pltpu.roll(h, nz - 1, 1) + h)
            flux_z = jnp.where(lane == nz - 1, 0.0, flux_z)
            flux_y = (pltpu.roll(p, ny - 1, 0) - p) / (pltpu.roll(h, ny - 1, 0) + h)
            flux_y = jnp.where(row == ny - 1, 0.0, flux_y)
            lap = (flux_z - pltpu.roll(flux_z, 1, 1)) + (flux_y - pltpu.roll(flux_y, 1, 0))
            right_ref[i * ny : (i + 1) * ny, :] = (lap - plane(source_ref, i, ny)) + ratio * p
        ratios = [plane(ratio_ref, i, ny) for i in range(nx)]
        halves = [plane(half_ref, i, ny) for i in range(nx)]
        _, up, down, ends = eliminate(ratios, halves, nx)
        for i in range(nx - 1):
            xup_ref[i] = up[i]
            xdown_ref[i] = down[i]
        for k in range(5):
            xends_ref[k] = ends[k]
        ratios = [rows_y(ratio_ref, j) for j in range(ny)]
        halves = [rows_y(half_ref, j) for j in range(ny)]
        _, up, down, ends = eliminate(ratios, halves, ny)
        for j in range(ny - 1):
            yup_ref[j] = up[j]
            ydown_ref[j] = down[j]
        for k in range(5):
            yends_ref[k] = ends[k]

    right0, ratio, xup, xdown, xends, yup, ydown, yends = call(
        inner_body,
        [
            (cells, nz), (cells, nz), (nx - 1, ny, nz), (nx - 1, ny, nz), (5, ny, nz),
            (ny - 1, nx, nz), (ny - 1, nx, nz), (5, nx, nz),
        ],
        [], pressure, source, porosity, half, name="inner",
    )

    def edges_body(
        right0_ref, p_ref, half_ref, far_ref, near_ref, xup_ref, xdown_ref, xends_ref, right_ref, send_ref
    ):
        place = lax.axis_index("gy")
        even = lax.rem(place, 2) == 0
        right_ref[...] = right0_ref[...]
        for j, is_end, low in ((0, place == 0, True), (ny - 1, place == count_gy - 1, False)):
            first, second = (far_ref, near_ref) if low else (near_ref, far_ref)
            other_h = jnp.where(even, first[0], second[0])
            other_p = jnp.where(even, first[1], second[1])
            flux = (other_p - rows_y(p_ref, j)) / (other_h + rows_y(half_ref, j))
            flux = jnp.where(is_end, 0.0, flux)
            right_ref[pl.ds(j, nx, stride=ny), :] = rows_y(right_ref, j) + flux
        right = [plane(right_ref, i, ny) for i in range(nx)]
        up = [xup_ref[i] for i in range(nx - 1)]
        down = [xdown_ref[i] for i in range(nx - 1)]
        first, last = offsets(right, up, down, xends_ref[3], xends_ref[4], nx)
        for k, value in enumerate((xends_ref[0], xends_ref[1], xends_ref[2], first, last)):
            for target in range(NEAR_X):
                send_ref[target, k] = value

    right, near_x = call(
        edges_body, [(cells, nz), (NEAR_X, 5, ny, nz)], [],
        right0, pressure, half, far_got, near_got, xup, xdown, xends, name="edges",
    )
    near_x = lax.all_to_all(near_x, "gx", 0, 0, axis_index_groups=near_x_groups)

    def ring_body(got_ref, send_ref, tree_ref):
        pieces = [tuple(got_ref[n, k] for k in range(5)) for n in range(NEAR_X)]
        merged, tree = join_all(pieces)
        for k in range(5):
            for target in range(far_x):
                send_ref[target, k] = merged[k]
        for k, value in enumerate(tree_values(tree)):
            tree_ref[k] = value

    far_x_send, x_tree = call(
        ring_body, [(far_x, 5, ny, nz), (3 * (NEAR_X - 1), ny, nz)], [], near_x, name="x_ring"
    )
    far_x_got = lax.all_to_all(far_x_send, "gx", 0, 0, axis_index_groups=far_x_groups)

    def along_x_body(
        got_ref, tree_ref, right_ref, half_ref, ratio_ref, p_ref, xup_ref, xends_ref,
        yup_ref, ydown_ref, yends_ref,
        send_ref, yright_ref, far_faces, near_faces, solved_ref,
    ):
        place = lax.axis_index("gx")
        far = place // NEAR_X
        near = lax.rem(place, NEAR_X)
        pieces = [tuple(got_ref[n, k] for k in range(5)) for n in range(far_x)]
        _, tree = join_all(pieces)
        fluxes = face_fluxes(tree, None, None)
        zero = jnp.zeros((ny, nz), F32)
        for k, value in enumerate(fluxes):
            far_faces[k] = zero if value is None else value
        low = far_faces[far]
        high = far_faces[far + 1]
        tree = tree_of(tree_shape(NEAR_X), [tree_ref[k] for k in range(3 * (NEAR_X - 1))])
        for k, value in enumerate(face_fluxes(tree, low, high)):
            near_faces[k] = value
        low = near_faces[near]
        high = near_faces[near + 1]
        gaps = [plane(half_ref, i, ny) + plane(half_ref, i + 1, ny) for i in range(nx - 1)]
        up = [xup_ref[i] for i in range(nx - 1)]
        right = [plane(right_ref, i, ny) for i in range(nx)]
        values = substitute(right, gaps, up, xends_ref[4], low, high, nx)
        for i in range(nx):
            solved_ref[i * ny : (i + 1) * ny, :] = plane(ratio_ref, i, ny) * (values[i] - plane(p_ref, i, ny))
        yright = [rows_y(solved_ref, j) for j in range(ny)]
        for j in range(ny):
            yright_ref[j] = yright[j]
        up = [yup_ref[j] for j in range(ny - 1)]
        down = [ydown_ref[j] for j in range(ny - 1)]
        first, last = offsets(yright, up, down, yends_ref[3], yends_ref[4], ny)
        for k, value in enumerate((yends_ref[0], yends_ref[1], yends_ref[2], first, last)):
            send_ref[k] = value

    pair_send, yright = call(
        along_x_body,
        [(5, nx, nz), (ny, nx, nz)],
        [(far_x + 1, ny, nz), (NEAR_X + 1, ny, nz), (cells, nz)],
        far_x_got, x_tree, right, half, ratio, pressure, xup, xends, yup, ydown, yends,
        name="along_x",
    )
    pair_got = lax.ppermute(pair_send, "gy", [(i, i ^ 1) for i in range(count_gy)])

    def pair_body(own_ref, got_ref, send_ref, tree_ref):
        even = lax.rem(lax.axis_index("gy"), 2) == 0
        left = tuple(jnp.where(even, own_ref[k], got_ref[k]) for k in range(5))
        right = tuple(jnp.where(even, got_ref[k], own_ref[k]) for k in range(5))
        merged, face = join(left, right)
        for k in range(5):
            for target in range(far_y):
                send_ref[target, k] = merged[k]
        for k in range(3):
            tree_ref[k] = face[k]

    far_y_send, y_tree = call(
        pair_body, [(far_y, 5, nx, nz), (3, nx, nz)], [], pair_send, pair_got, name="y_pair"
    )
    far_y_got = lax.all_to_all(far_y_send, "gy", 0, 0, axis_index_groups=far_y_groups)

    def updated_body(
        got_ref, tree_ref, yright_ref, half_ref, p_ref, yup_ref, yends_ref, out_ref, far_faces, near_faces
    ):
        place = lax.axis_index("gy")
        far = place // NEAR_Y
        near = lax.rem(place, NEAR_Y)
        pieces = [tuple(got_ref[n, k] for k in range(5)) for n in range(far_y)]
        _, tree = join_all(pieces)
        zero = jnp.zeros((nx, nz), F32)
        for k, value in enumerate(face_fluxes(tree, None, None)):
            far_faces[k] = zero if value is None else value
        low = far_faces[far]
        high = far_faces[far + 1]
        tree = tree_of(tree_shape(NEAR_Y), [tree_ref[k] for k in range(3)])
        for k, value in enumerate(face_fluxes(tree, low, high)):
            near_faces[k] = value
        low = near_faces[near]
        high = near_faces[near + 1]
        halves = [rows_y(half_ref, j) for j in range(ny)]
        gaps = [halves[j] + halves[j + 1] for j in range(ny - 1)]
        up = [yup_ref[j] for j in range(ny - 1)]
        right = [yright_ref[j] for j in range(ny)]
        values = substitute(right, gaps, up, yends_ref[4], low, high, ny)
        for j in range(ny):
            out_ref[pl.ds(j, nx, stride=ny), :] = rows_y(p_ref, j) + values[j]

    (updated,) = call(
        updated_body,
        [(cells, nz)],
        [(far_y + 1, nx, nz), (NEAR_Y + 1, nx, nz)],
        far_y_got, y_tree, yright, half, pressure, yup, yends,
        name="updated",
    )
    return updated.reshape(nx, ny, nz)


def solution(mesh):
    spec = P("gx", "gy", None)
    sizes_mesh = (mesh.shape["gx"], mesh.shape["gy"])

    def local(pressure, source, porosity, permeability, speed):
        return local_step(
            pressure.shape, sizes_mesh, pressure, source, porosity, permeability, speed
        )

    return jax.shard_map(
        local, mesh=mesh, in_specs=(spec,) * 5, out_specs=spec, check_vma=False
    )
```

```python
import jax
import jax.numpy as jnp
from jax import lax
from jax.experimental import pallas as pl
from jax.experimental.pallas import tpu as pltpu
from jax.sharding import PartitionSpec as P

FORCH = 0.55
STEP = 500.0
NEAR_X = 4
NEAR_Y = 2
F32 = jnp.float32


def join(left, right):
    la, lb, lc, lg, lh = left
    ra, rb, rc, rg, rh = right
    inv = 1.0 / (lc + ra)
    left_share = lb * inv
    right_share = rb * inv
    gap = lh - rg
    merged = (
        la - lb * left_share,
        lb * right_share,
        rc - rb * right_share,
        lg - left_share * gap,
        rh + right_share * gap,
    )
    return merged, (inv * gap, left_share, right_share)


def join_all(pieces):
    if len(pieces) == 1:
        return pieces[0], None
    half = len(pieces) // 2
    left, left_tree = join_all(pieces[:half])
    right, right_tree = join_all(pieces[half:])
    merged, face = join(left, right)
    return merged, (face, left_tree, right_tree)


def face_fluxes(tree, low, high):
    if tree is None:
        return [low, high]
    face, left_tree, right_tree = tree
    flux = face[0]
    if low is not None:
        flux = flux + face[1] * low
    if high is not None:
        flux = flux + face[2] * high
    return face_fluxes(left_tree, low, flux) + face_fluxes(right_tree, flux, high)[1:]


def tree_shape(count):
    if count == 1:
        return None
    return (count, tree_shape(count // 2), tree_shape(count // 2))


def tree_values(tree):
    if tree is None:
        return []
    return list(tree[0]) + tree_values(tree[1]) + tree_values(tree[2])


def tree_of(shape, values):
    if shape is None:
        return None
    face = tuple(values.pop(0) for _ in range(3))
    left = tree_of(shape[1], values)
    return (face, left, tree_of(shape[2], values))


def plane(ref, i, rows):
    return ref[i * rows : (i + 1) * rows, :]


def eliminate(ratio, half, count):
    gaps = [half[i] + half[i + 1] for i in range(count - 1)]
    up = []
    total = ratio[0]
    for i in range(count - 1):
        carry = 1.0 / (1.0 + total * gaps[i])
        up.append(carry)
        total = ratio[i + 1] + total * carry
    last_inv = 1.0 / total
    down = [None] * (count - 1)
    total = ratio[count - 1]
    for i in range(count - 2, -1, -1):
        carry = 1.0 / (1.0 + total * gaps[i])
        down[i] = carry
        total = ratio[i] + total * carry
    first_inv = 1.0 / total
    across = last_inv
    for i in range(count - 2, -1, -1):
        across = across * up[i]
    ends = [first_inv + half[0], across, last_inv + half[count - 1], first_inv, last_inv]
    return gaps, up, down, ends


def offsets(right, up, down, first_inv, last_inv, count):
    rising = right[0]
    for i in range(count - 1):
        rising = right[i + 1] + up[i] * rising
    falling = right[count - 1]
    for i in range(count - 2, -1, -1):
        falling = right[i] + down[i] * falling
    return falling * first_inv, rising * last_inv


def substitute(right, gaps, up, last_inv, low, high, count):
    sums = [right[0] + low]
    for i in range(count - 1):
        sums.append(right[i + 1] + up[i] * sums[i])
    values = [None] * count
    values[count - 1] = (sums[count - 1] - high) * last_inv
    for i in range(count - 2, -1, -1):
        values[i] = up[i] * (values[i + 1] + gaps[i] * sums[i])
    return values


def local_step(sizes, sizes_mesh, pressure, source, porosity, permeability, speed):
    nx, ny, nz = sizes
    count_gx, count_gy = sizes_mesh
    far_x = count_gx // NEAR_X
    far_y = count_gy // NEAR_Y
    near_x_groups = [[z * NEAR_X + x for x in range(NEAR_X)] for z in range(far_x)]
    far_x_groups = [[z * NEAR_X + x for z in range(far_x)] for x in range(NEAR_X)]
    near_y_groups = [[y * NEAR_Y + c for c in range(NEAR_Y)] for y in range(far_y)]
    far_y_groups = [[y * NEAR_Y + c for y in range(far_y)] for c in range(NEAR_Y)]
    cells = nx * ny
    pressure = pressure.reshape(cells, nz)
    source = source.reshape(cells, nz)
    porosity = porosity.reshape(cells, nz)
    permeability = permeability.reshape(cells, nz)
    speed = speed.reshape(cells, nz)

    def call(body, shapes, scratch, *args, name):
        return pl.pallas_call(
            body,
            out_shape=[jax.ShapeDtypeStruct(s, F32) for s in shapes],
            in_specs=[pl.BlockSpec(memory_space=pltpu.VMEM)] * len(args),
            out_specs=[pl.BlockSpec(memory_space=pltpu.VMEM)] * len(shapes),
            scratch_shapes=[pltpu.VMEM(s, F32) for s in scratch],
            compiler_params=pltpu.CompilerParams(vmem_limit_bytes=32 * 1024 * 1024),
            name=name,
        )(*args)

    def rows_y(ref, j):
        return ref[pl.ds(j, nx, stride=ny), :]

    def halves_body(
        p_hbm, source_hbm, por_hbm, perm_hbm, speed_hbm,
        half_ref, near_ref, far_ref, p_ref, source_ref, por_ref, perm_ref, speed_ref, sems,
    ):
        pairs = (
            (perm_hbm, perm_ref), (speed_hbm, speed_ref), (p_hbm, p_ref),
            (source_hbm, source_ref), (por_hbm, por_ref),
        )
        copies = [pltpu.make_async_copy(a, b, sems.at[n]) for n, (a, b) in enumerate(pairs)]
        for copy in copies:
            copy.start()
        for copy in copies[:3]:
            copy.wait()
        for i in range(nx):
            root = lax.rsqrt(plane(perm_ref, i, ny).astype(F32))
            half_ref[i * ny : (i + 1) * ny, :] = (0.5 * root) * (
                root + FORCH * plane(speed_ref, i, ny).astype(F32)
            )
        even = lax.rem(lax.axis_index("gy"), 2) == 0
        for k, ref in enumerate((half_ref, p_ref)):
            low = rows_y(ref, 0)
            high = rows_y(ref, ny - 1)
            near_ref[k] = jnp.where(even, high, low)
            far_ref[k] = jnp.where(even, low, high)
        for copy in copies[3:]:
            copy.wait()

    vmem = pl.BlockSpec(memory_space=pltpu.VMEM)
    half, near_send, far_send, pressure, source, porosity = pl.pallas_call(
        halves_body,
        out_shape=[
            jax.ShapeDtypeStruct((cells, nz), F32),
            jax.ShapeDtypeStruct((2, nx, nz), F32),
            jax.ShapeDtypeStruct((2, nx, nz), F32),
            jax.ShapeDtypeStruct((cells, nz), F32),
            jax.ShapeDtypeStruct((cells, nz), F32),
            jax.ShapeDtypeStruct((cells, nz), porosity.dtype),
        ],
        in_specs=[pl.BlockSpec(memory_space=pltpu.HBM)] * 5,
        out_specs=[vmem] * 6,
        scratch_shapes=[
            pltpu.VMEM((cells, nz), permeability.dtype),
            pltpu.VMEM((cells, nz), speed.dtype),
            pltpu.SemaphoreType.DMA((5,)),
        ],
        compiler_params=pltpu.CompilerParams(vmem_limit_bytes=16 * 1024 * 1024),
        name="halves",
    )(*(pltpu.with_memory_space_constraint(a, pltpu.HBM) for a in (pressure, source, porosity, permeability, speed)))
    far_pairs = []
    for i in range(1, count_gy - 1, 2):
        far_pairs += [(i, i + 1), (i + 1, i)]
    far_got = lax.ppermute(far_send, "gy", far_pairs)
    near_got = lax.all_gather(near_send, "gy", axis=0, axis_index_groups=near_y_groups)

    def inner_body(
        p_ref, source_ref, por_ref, half_ref,
        right_ref, ratio_ref, xup_ref, xdown_ref, xends_ref, yup_ref, ydown_ref, yends_ref,
    ):
        lane = lax.broadcasted_iota(jnp.int32, (ny, nz), 1)
        row = lax.broadcasted_iota(jnp.int32, (ny, nz), 0)
        for i in range(nx):
            p = plane(p_ref, i, ny)
            h = plane(half_ref, i, ny)
            ratio = plane(por_ref, i, ny).astype(F32) * (1.0 / STEP)
            ratio_ref[i * ny : (i + 1) * ny, :] = ratio
            flux_z = (pltpu.roll(p, nz - 1, 1) - p) / (pltpu.roll(h, nz - 1, 1) + h)
            flux_z = jnp.where(lane == nz - 1, 0.0, flux_z)
            flux_y = (pltpu.roll(p, ny - 1, 0) - p) / (pltpu.roll(h, ny - 1, 0) + h)
            flux_y = jnp.where(row == ny - 1, 0.0, flux_y)
            lap = (flux_z - pltpu.roll(flux_z, 1, 1)) + (flux_y - pltpu.roll(flux_y, 1, 0))
            right_ref[i * ny : (i + 1) * ny, :] = (lap - plane(source_ref, i, ny)) + ratio * p
        ratios = [plane(ratio_ref, i, ny) for i in range(nx)]
        halves = [plane(half_ref, i, ny) for i in range(nx)]
        _, up, down, ends = eliminate(ratios, halves, nx)
        for i in range(nx - 1):
            xup_ref[i] = up[i]
            xdown_ref[i] = down[i]
        for k in range(5):
            xends_ref[k] = ends[k]
        ratios = [rows_y(ratio_ref, j) for j in range(ny)]
        halves = [rows_y(half_ref, j) for j in range(ny)]
        _, up, down, ends = eliminate(ratios, halves, ny)
        for j in range(ny - 1):
            yup_ref[j] = up[j]
            ydown_ref[j] = down[j]
        for k in range(5):
            yends_ref[k] = ends[k]

    right0, ratio, xup, xdown, xends, yup, ydown, yends = call(
        inner_body,
        [
            (cells, nz), (cells, nz), (nx - 1, ny, nz), (nx - 1, ny, nz), (5, ny, nz),
            (ny - 1, nx, nz), (ny - 1, nx, nz), (5, nx, nz),
        ],
        [], pressure, source, porosity, half, name="inner",
    )

    def edges_body(
        right0_ref, p_ref, half_ref, far_ref, near_ref, xup_ref, xdown_ref, xends_ref, right_ref, send_ref
    ):
        place = lax.axis_index("gy")
        even = lax.rem(place, 2) == 0
        right_ref[...] = right0_ref[...]
        for j, is_end, low in ((0, place == 0, True), (ny - 1, place == count_gy - 1, False)):
            other_h, other_p = (
                jnp.where(even, far_ref[k], near_ref[0, k]) if low else jnp.where(even, near_ref[1, k], far_ref[k])
                for k in range(2)
            )
            flux = (other_p - rows_y(p_ref, j)) / (other_h + rows_y(half_ref, j))
            flux = jnp.where(is_end, 0.0, flux)
            right_ref[pl.ds(j, nx, stride=ny), :] = rows_y(right_ref, j) + flux
        right = [plane(right_ref, i, ny) for i in range(nx)]
        up = [xup_ref[i] for i in range(nx - 1)]
        down = [xdown_ref[i] for i in range(nx - 1)]
        first, last = offsets(right, up, down, xends_ref[3], xends_ref[4], nx)
        for k, value in enumerate((xends_ref[0], xends_ref[1], xends_ref[2], first, last)):
            for target in range(NEAR_X):
                send_ref[target, k] = value

    right, near_x = call(
        edges_body, [(cells, nz), (NEAR_X, 5, ny, nz)], [],
        right0, pressure, half, far_got, near_got, xup, xdown, xends, name="edges",
    )
    near_x = lax.all_to_all(near_x, "gx", 0, 0, axis_index_groups=near_x_groups)

    def ring_body(got_ref, send_ref, tree_ref):
        pieces = [tuple(got_ref[n, k] for k in range(5)) for n in range(NEAR_X)]
        merged, tree = join_all(pieces)
        for k in range(5):
            for target in range(far_x):
                send_ref[target, k] = merged[k]
        for k, value in enumerate(tree_values(tree)):
            tree_ref[k] = value

    far_x_send, x_tree = call(
        ring_body, [(far_x, 5, ny, nz), (3 * (NEAR_X - 1), ny, nz)], [], near_x, name="x_ring"
    )
    far_x_got = lax.all_to_all(far_x_send, "gx", 0, 0, axis_index_groups=far_x_groups)

    def along_x_body(
        got_ref, tree_ref, right_ref, half_ref, ratio_ref, p_ref, xup_ref, xends_ref,
        yup_ref, ydown_ref, yends_ref,
        send_ref, yright_ref, far_faces, near_faces, solved_ref,
    ):
        place = lax.axis_index("gx")
        far = place // NEAR_X
        near = lax.rem(place, NEAR_X)
        pieces = [tuple(got_ref[n, k] for k in range(5)) for n in range(far_x)]
        _, tree = join_all(pieces)
        fluxes = face_fluxes(tree, None, None)
        zero = jnp.zeros((ny, nz), F32)
        for k, value in enumerate(fluxes):
            far_faces[k] = zero if value is None else value
        low = far_faces[far]
        high = far_faces[far + 1]
        tree = tree_of(tree_shape(NEAR_X), [tree_ref[k] for k in range(3 * (NEAR_X - 1))])
        for k, value in enumerate(face_fluxes(tree, low, high)):
            near_faces[k] = value
        low = near_faces[near]
        high = near_faces[near + 1]
        gaps = [plane(half_ref, i, ny) + plane(half_ref, i + 1, ny) for i in range(nx - 1)]
        up = [xup_ref[i] for i in range(nx - 1)]
        right = [plane(right_ref, i, ny) for i in range(nx)]
        values = substitute(right, gaps, up, xends_ref[4], low, high, nx)
        for i in range(nx):
            solved_ref[i * ny : (i + 1) * ny, :] = plane(ratio_ref, i, ny) * (values[i] - plane(p_ref, i, ny))
        yright = [rows_y(solved_ref, j) for j in range(ny)]
        for j in range(ny):
            yright_ref[j] = yright[j]
        up = [yup_ref[j] for j in range(ny - 1)]
        down = [ydown_ref[j] for j in range(ny - 1)]
        first, last = offsets(yright, up, down, yends_ref[3], yends_ref[4], ny)
        for k, value in enumerate((yends_ref[0], yends_ref[1], yends_ref[2], first, last)):
            send_ref[k] = value

    pair_send, yright = call(
        along_x_body,
        [(5, nx, nz), (ny, nx, nz)],
        [(far_x + 1, ny, nz), (NEAR_X + 1, ny, nz), (cells, nz)],
        far_x_got, x_tree, right, half, ratio, pressure, xup, xends, yup, ydown, yends,
        name="along_x",
    )
    pair_got = lax.all_gather(pair_send, "gy", axis=0, axis_index_groups=near_y_groups)

    def pair_body(got_ref, send_ref, tree_ref):
        left, right = (tuple(got_ref[n, k] for k in range(5)) for n in range(NEAR_Y))
        merged, face = join(left, right)
        for k in range(5):
            for target in range(far_y):
                send_ref[target, k] = merged[k]
        for k in range(3):
            tree_ref[k] = face[k]

    far_y_send, y_tree = call(
        pair_body, [(far_y, 5, nx, nz), (3, nx, nz)], [], pair_got, name="y_pair"
    )
    far_y_got = lax.all_to_all(far_y_send, "gy", 0, 0, axis_index_groups=far_y_groups)

    def updated_body(
        got_ref, tree_ref, yright_ref, half_ref, p_ref, yup_ref, yends_ref, out_ref, far_faces, near_faces
    ):
        place = lax.axis_index("gy")
        far = place // NEAR_Y
        near = lax.rem(place, NEAR_Y)
        pieces = [tuple(got_ref[n, k] for k in range(5)) for n in range(far_y)]
        _, tree = join_all(pieces)
        zero = jnp.zeros((nx, nz), F32)
        for k, value in enumerate(face_fluxes(tree, None, None)):
            far_faces[k] = zero if value is None else value
        low = far_faces[far]
        high = far_faces[far + 1]
        tree = tree_of(tree_shape(NEAR_Y), [tree_ref[k] for k in range(3)])
        for k, value in enumerate(face_fluxes(tree, low, high)):
            near_faces[k] = value
        low = near_faces[near]
        high = near_faces[near + 1]
        halves = [rows_y(half_ref, j) for j in range(ny)]
        gaps = [halves[j] + halves[j + 1] for j in range(ny - 1)]
        up = [yup_ref[j] for j in range(ny - 1)]
        right = [yright_ref[j] for j in range(ny)]
        values = substitute(right, gaps, up, yends_ref[4], low, high, ny)
        for j in range(ny):
            out_ref[pl.ds(j, nx, stride=ny), :] = rows_y(p_ref, j) + values[j]

    (updated,) = call(
        updated_body,
        [(cells, nz)],
        [(far_y + 1, nx, nz), (NEAR_Y + 1, nx, nz)],
        far_y_got, y_tree, yright, half, pressure, yup, yends,
        name="updated",
    )
    return updated.reshape(nx, ny, nz)


def solution(mesh):
    spec = P("gx", "gy", None)
    sizes_mesh = (mesh.shape["gx"], mesh.shape["gy"])

    def local(pressure, source, porosity, permeability, speed):
        return local_step(
            pressure.shape, sizes_mesh, pressure, source, porosity, permeability, speed
        )

    return jax.shard_map(
        local, mesh=mesh, in_specs=(spec,) * 5, out_specs=spec, check_vma=False
    )
```

```python
import jax
import jax.numpy as jnp
from jax import lax
from jax.experimental import pallas as pl
from jax.experimental.pallas import tpu as pltpu
from jax.sharding import PartitionSpec as P

FORCH = 0.55
STEP = 500.0
NEAR_X = 8
NEAR_Y = 4
F32 = jnp.float32


def join(left, right):
    la, lb, lc, lg, lh = left
    ra, rb, rc, rg, rh = right
    inv = 1.0 / (lc + ra)
    left_share = lb * inv
    right_share = rb * inv
    gap = lh - rg
    merged = (
        la - lb * left_share,
        lb * right_share,
        rc - rb * right_share,
        lg - left_share * gap,
        rh + right_share * gap,
    )
    return merged, (inv * gap, left_share, right_share)


def join_all(pieces):
    if len(pieces) == 1:
        return pieces[0], None
    half = len(pieces) // 2
    left, left_tree = join_all(pieces[:half])
    right, right_tree = join_all(pieces[half:])
    merged, face = join(left, right)
    return merged, (face, left_tree, right_tree)


def face_fluxes(tree, low, high):
    if tree is None:
        return [low, high]
    face, left_tree, right_tree = tree
    flux = face[0]
    if low is not None:
        flux = flux + face[1] * low
    if high is not None:
        flux = flux + face[2] * high
    return face_fluxes(left_tree, low, flux) + face_fluxes(right_tree, flux, high)[1:]


def tree_shape(count):
    if count == 1:
        return None
    return (count, tree_shape(count // 2), tree_shape(count // 2))


def tree_values(tree):
    if tree is None:
        return []
    return list(tree[0]) + tree_values(tree[1]) + tree_values(tree[2])


def tree_of(shape, values):
    if shape is None:
        return None
    face = tuple(values.pop(0) for _ in range(3))
    left = tree_of(shape[1], values)
    return (face, left, tree_of(shape[2], values))


def plane(ref, i, rows):
    return ref[i * rows : (i + 1) * rows, :]


def eliminate(ratio, half, count):
    gaps = [half[i] + half[i + 1] for i in range(count - 1)]
    up = []
    total = ratio[0]
    for i in range(count - 1):
        carry = 1.0 / (1.0 + total * gaps[i])
        up.append(carry)
        total = ratio[i + 1] + total * carry
    last_inv = 1.0 / total
    down = [None] * (count - 1)
    total = ratio[count - 1]
    for i in range(count - 2, -1, -1):
        carry = 1.0 / (1.0 + total * gaps[i])
        down[i] = carry
        total = ratio[i] + total * carry
    first_inv = 1.0 / total
    across = last_inv
    for i in range(count - 2, -1, -1):
        across = across * up[i]
    ends = [first_inv + half[0], across, last_inv + half[count - 1], first_inv, last_inv]
    return gaps, up, down, ends


def offsets(right, up, down, first_inv, last_inv, count):
    rising = right[0]
    for i in range(count - 1):
        rising = right[i + 1] + up[i] * rising
    falling = right[count - 1]
    for i in range(count - 2, -1, -1):
        falling = right[i] + down[i] * falling
    return falling * first_inv, rising * last_inv


def substitute(right, gaps, up, last_inv, low, high, count):
    sums = [right[0] + low]
    for i in range(count - 1):
        sums.append(right[i + 1] + up[i] * sums[i])
    values = [None] * count
    values[count - 1] = (sums[count - 1] - high) * last_inv
    for i in range(count - 2, -1, -1):
        values[i] = up[i] * (values[i + 1] + gaps[i] * sums[i])
    return values


def local_step(sizes, sizes_mesh, pressure, source, porosity, permeability, speed):
    nx, ny, nz = sizes
    count_gx, count_gy = sizes_mesh
    far_x = count_gx // NEAR_X
    far_y = count_gy // NEAR_Y
    near_x_groups = [[z * NEAR_X + x for x in range(NEAR_X)] for z in range(far_x)]
    far_x_groups = [[z * NEAR_X + x for z in range(far_x)] for x in range(NEAR_X)]
    near_y_groups = [[y * NEAR_Y + c for c in range(NEAR_Y)] for y in range(far_y)]
    chip_groups = [[y, y + 1] for y in range(0, count_gy, 2)]
    far_y_groups = [[y * NEAR_Y + c for y in range(far_y)] for c in range(NEAR_Y)]
    cells = nx * ny
    pressure = pressure.reshape(cells, nz)
    source = source.reshape(cells, nz)
    porosity = porosity.reshape(cells, nz)
    permeability = permeability.reshape(cells, nz)
    speed = speed.reshape(cells, nz)

    def call(body, shapes, scratch, *args, name):
        return pl.pallas_call(
            body,
            out_shape=[jax.ShapeDtypeStruct(s, F32) for s in shapes],
            in_specs=[pl.BlockSpec(memory_space=pltpu.VMEM)] * len(args),
            out_specs=[pl.BlockSpec(memory_space=pltpu.VMEM)] * len(shapes),
            scratch_shapes=[pltpu.VMEM(s, F32) for s in scratch],
            compiler_params=pltpu.CompilerParams(vmem_limit_bytes=32 * 1024 * 1024),
            name=name,
        )(*args)

    def rows_y(ref, j):
        return ref[pl.ds(j, nx, stride=ny), :]

    def halves_body(
        p_hbm, source_hbm, por_hbm, perm_hbm, speed_hbm,
        half_ref, near_ref, far_ref, p_ref, source_ref, por_ref, perm_ref, speed_ref, sems,
    ):
        pairs = (
            (perm_hbm, perm_ref), (speed_hbm, speed_ref), (p_hbm, p_ref),
            (source_hbm, source_ref), (por_hbm, por_ref),
        )
        copies = [pltpu.make_async_copy(a, b, sems.at[n]) for n, (a, b) in enumerate(pairs)]
        for copy in copies:
            copy.start()
        for copy in copies[:3]:
            copy.wait()
        for i in range(nx):
            root = lax.rsqrt(plane(perm_ref, i, ny).astype(F32))
            half_ref[i * ny : (i + 1) * ny, :] = (0.5 * root) * (
                root + FORCH * plane(speed_ref, i, ny).astype(F32)
            )
        even = lax.rem(lax.axis_index("gy"), 2) == 0
        for k, ref in enumerate((half_ref, p_ref)):
            low = rows_y(ref, 0)
            high = rows_y(ref, ny - 1)
            near_ref[k] = jnp.where(even, high, low)
            far_ref[k] = jnp.where(even, low, high)
        for copy in copies[3:]:
            copy.wait()

    vmem = pl.BlockSpec(memory_space=pltpu.VMEM)
    half, near_send, far_send, pressure, source, porosity = pl.pallas_call(
        halves_body,
        out_shape=[
            jax.ShapeDtypeStruct((cells, nz), F32),
            jax.ShapeDtypeStruct((2, nx, nz), F32),
            jax.ShapeDtypeStruct((2, nx, nz), F32),
            jax.ShapeDtypeStruct((cells, nz), F32),
            jax.ShapeDtypeStruct((cells, nz), F32),
            jax.ShapeDtypeStruct((cells, nz), porosity.dtype),
        ],
        in_specs=[pl.BlockSpec(memory_space=pltpu.HBM)] * 5,
        out_specs=[vmem] * 6,
        scratch_shapes=[
            pltpu.VMEM((cells, nz), permeability.dtype),
            pltpu.VMEM((cells, nz), speed.dtype),
            pltpu.SemaphoreType.DMA((5,)),
        ],
        compiler_params=pltpu.CompilerParams(vmem_limit_bytes=16 * 1024 * 1024),
        name="halves",
    )(*(pltpu.with_memory_space_constraint(a, pltpu.HBM) for a in (pressure, source, porosity, permeability, speed)))
    far_pairs = []
    for i in range(1, count_gy - 1, 2):
        far_pairs += [(i, i + 1), (i + 1, i)]
    far_got = lax.ppermute(far_send, "gy", far_pairs)
    near_got = lax.all_gather(near_send, "gy", axis=0, axis_index_groups=chip_groups)

    def inner_body(
        p_ref, source_ref, por_ref, half_ref,
        right_ref, ratio_ref, xup_ref, xdown_ref, xends_ref, yup_ref, ydown_ref, yends_ref,
    ):
        lane = lax.broadcasted_iota(jnp.int32, (ny, nz), 1)
        row = lax.broadcasted_iota(jnp.int32, (ny, nz), 0)
        for i in range(nx):
            p = plane(p_ref, i, ny)
            h = plane(half_ref, i, ny)
            ratio = plane(por_ref, i, ny).astype(F32) * (1.0 / STEP)
            ratio_ref[i * ny : (i + 1) * ny, :] = ratio
            flux_z = (pltpu.roll(p, nz - 1, 1) - p) / (pltpu.roll(h, nz - 1, 1) + h)
            flux_z = jnp.where(lane == nz - 1, 0.0, flux_z)
            flux_y = (pltpu.roll(p, ny - 1, 0) - p) / (pltpu.roll(h, ny - 1, 0) + h)
            flux_y = jnp.where(row == ny - 1, 0.0, flux_y)
            lap = (flux_z - pltpu.roll(flux_z, 1, 1)) + (flux_y - pltpu.roll(flux_y, 1, 0))
            right_ref[i * ny : (i + 1) * ny, :] = (lap - plane(source_ref, i, ny)) + ratio * p
        ratios = [plane(ratio_ref, i, ny) for i in range(nx)]
        halves = [plane(half_ref, i, ny) for i in range(nx)]
        _, up, down, ends = eliminate(ratios, halves, nx)
        for i in range(nx - 1):
            xup_ref[i] = up[i]
            xdown_ref[i] = down[i]
        for k in range(5):
            xends_ref[k] = ends[k]
        ratios = [rows_y(ratio_ref, j) for j in range(ny)]
        halves = [rows_y(half_ref, j) for j in range(ny)]
        _, up, down, ends = eliminate(ratios, halves, ny)
        for j in range(ny - 1):
            yup_ref[j] = up[j]
            ydown_ref[j] = down[j]
        for k in range(5):
            yends_ref[k] = ends[k]

    right0, ratio, xup, xdown, xends, yup, ydown, yends = call(
        inner_body,
        [
            (cells, nz), (cells, nz), (nx - 1, ny, nz), (nx - 1, ny, nz), (5, ny, nz),
            (ny - 1, nx, nz), (ny - 1, nx, nz), (5, nx, nz),
        ],
        [], pressure, source, porosity, half, name="inner",
    )

    def edges_body(
        right0_ref, p_ref, half_ref, far_ref, near_ref, xup_ref, xdown_ref, xends_ref, right_ref, send_ref
    ):
        place = lax.axis_index("gy")
        even = lax.rem(place, 2) == 0
        right_ref[...] = right0_ref[...]
        for j, is_end, low in ((0, place == 0, True), (ny - 1, place == count_gy - 1, False)):
            other_h, other_p = (
                jnp.where(even, far_ref[k], near_ref[0, k]) if low else jnp.where(even, near_ref[1, k], far_ref[k])
                for k in range(2)
            )
            flux = (other_p - rows_y(p_ref, j)) / (other_h + rows_y(half_ref, j))
            flux = jnp.where(is_end, 0.0, flux)
            right_ref[pl.ds(j, nx, stride=ny), :] = rows_y(right_ref, j) + flux
        right = [plane(right_ref, i, ny) for i in range(nx)]
        up = [xup_ref[i] for i in range(nx - 1)]
        down = [xdown_ref[i] for i in range(nx - 1)]
        first, last = offsets(right, up, down, xends_ref[3], xends_ref[4], nx)
        for k, value in enumerate((xends_ref[0], xends_ref[1], xends_ref[2], first, last)):
            for target in range(NEAR_X):
                send_ref[target, k] = value

    right, near_x = call(
        edges_body, [(cells, nz), (NEAR_X, 5, ny, nz)], [],
        right0, pressure, half, far_got, near_got, xup, xdown, xends, name="edges",
    )
    near_x = lax.all_to_all(near_x, "gx", 0, 0, axis_index_groups=near_x_groups)

    def ring_body(got_ref, send_ref, tree_ref):
        pieces = [tuple(got_ref[n, k] for k in range(5)) for n in range(NEAR_X)]
        merged, tree = join_all(pieces)
        for k in range(5):
            for target in range(far_x):
                send_ref[target, k] = merged[k]
        for k, value in enumerate(tree_values(tree)):
            tree_ref[k] = value

    far_x_send, x_tree = call(
        ring_body, [(far_x, 5, ny, nz), (3 * (NEAR_X - 1), ny, nz)], [], near_x, name="x_ring"
    )
    far_x_got = lax.all_to_all(far_x_send, "gx", 0, 0, axis_index_groups=far_x_groups)

    def along_x_body(
        got_ref, tree_ref, right_ref, half_ref, ratio_ref, p_ref, xup_ref, xends_ref,
        yup_ref, ydown_ref, yends_ref,
        send_ref, yright_ref, far_faces, near_faces, solved_ref,
    ):
        place = lax.axis_index("gx")
        far = place // NEAR_X
        near = lax.rem(place, NEAR_X)
        pieces = [tuple(got_ref[n, k] for k in range(5)) for n in range(far_x)]
        _, tree = join_all(pieces)
        fluxes = face_fluxes(tree, None, None)
        zero = jnp.zeros((ny, nz), F32)
        for k, value in enumerate(fluxes):
            far_faces[k] = zero if value is None else value
        low = far_faces[far]
        high = far_faces[far + 1]
        tree = tree_of(tree_shape(NEAR_X), [tree_ref[k] for k in range(3 * (NEAR_X - 1))])
        for k, value in enumerate(face_fluxes(tree, low, high)):
            near_faces[k] = value
        low = near_faces[near]
        high = near_faces[near + 1]
        gaps = [plane(half_ref, i, ny) + plane(half_ref, i + 1, ny) for i in range(nx - 1)]
        up = [xup_ref[i] for i in range(nx - 1)]
        right = [plane(right_ref, i, ny) for i in range(nx)]
        values = substitute(right, gaps, up, xends_ref[4], low, high, nx)
        for i in range(nx):
            solved_ref[i * ny : (i + 1) * ny, :] = plane(ratio_ref, i, ny) * (values[i] - plane(p_ref, i, ny))
        yright = [rows_y(solved_ref, j) for j in range(ny)]
        for j in range(ny):
            yright_ref[j] = yright[j]
        up = [yup_ref[j] for j in range(ny - 1)]
        down = [ydown_ref[j] for j in range(ny - 1)]
        first, last = offsets(yright, up, down, yends_ref[3], yends_ref[4], ny)
        for k, value in enumerate((yends_ref[0], yends_ref[1], yends_ref[2], first, last)):
            send_ref[k] = value

    pair_send, yright = call(
        along_x_body,
        [(5, nx, nz), (ny, nx, nz)],
        [(far_x + 1, ny, nz), (NEAR_X + 1, ny, nz), (cells, nz)],
        far_x_got, x_tree, right, half, ratio, pressure, xup, xends, yup, ydown, yends,
        name="along_x",
    )
    pair_got = lax.all_gather(pair_send, "gy", axis=0, axis_index_groups=near_y_groups)

    def pair_body(got_ref, send_ref, tree_ref):
        pieces = [tuple(got_ref[n, k] for k in range(5)) for n in range(NEAR_Y)]
        merged, tree = join_all(pieces)
        for k in range(5):
            for target in range(far_y):
                send_ref[target, k] = merged[k]
        for k, value in enumerate(tree_values(tree)):
            tree_ref[k] = value

    far_y_send, y_tree = call(
        pair_body, [(far_y, 5, nx, nz), (3 * (NEAR_Y - 1), nx, nz)], [], pair_got, name="y_pair"
    )
    far_y_got = lax.all_to_all(far_y_send, "gy", 0, 0, axis_index_groups=far_y_groups)

    def updated_body(
        got_ref, tree_ref, yright_ref, half_ref, p_ref, yup_ref, yends_ref, out_ref, far_faces, near_faces
    ):
        place = lax.axis_index("gy")
        far = place // NEAR_Y
        near = lax.rem(place, NEAR_Y)
        pieces = [tuple(got_ref[n, k] for k in range(5)) for n in range(far_y)]
        _, tree = join_all(pieces)
        zero = jnp.zeros((nx, nz), F32)
        for k, value in enumerate(face_fluxes(tree, None, None)):
            far_faces[k] = zero if value is None else value
        low = far_faces[far]
        high = far_faces[far + 1]
        tree = tree_of(tree_shape(NEAR_Y), [tree_ref[k] for k in range(3 * (NEAR_Y - 1))])
        for k, value in enumerate(face_fluxes(tree, low, high)):
            near_faces[k] = value
        low = near_faces[near]
        high = near_faces[near + 1]
        halves = [rows_y(half_ref, j) for j in range(ny)]
        gaps = [halves[j] + halves[j + 1] for j in range(ny - 1)]
        up = [yup_ref[j] for j in range(ny - 1)]
        right = [yright_ref[j] for j in range(ny)]
        values = substitute(right, gaps, up, yends_ref[4], low, high, ny)
        for j in range(ny):
            out_ref[pl.ds(j, nx, stride=ny), :] = rows_y(p_ref, j) + values[j]

    (updated,) = call(
        updated_body,
        [(cells, nz)],
        [(far_y + 1, nx, nz), (NEAR_Y + 1, nx, nz)],
        far_y_got, y_tree, yright, half, pressure, yup, yends,
        name="updated",
    )
    return updated.reshape(nx, ny, nz)


def solution(mesh):
    spec = P("gx", "gy", None)
    sizes_mesh = (mesh.shape["gx"], mesh.shape["gy"])

    def local(pressure, source, porosity, permeability, speed):
        return local_step(
            pressure.shape, sizes_mesh, pressure, source, porosity, permeability, speed
        )

    return jax.shard_map(
        local, mesh=mesh, in_specs=(spec,) * 5, out_specs=spec, check_vma=False
    )
```

```python
import jax
import jax.numpy as jnp
from jax import lax
from jax.experimental import pallas as pl
from jax.experimental.pallas import tpu as pltpu
from jax.sharding import PartitionSpec as P

FORCH = 0.55
STEP = 500.0
RING_X = 4
CORES = 2
NEAR_X = 2 * RING_X
NEAR_Y = 2 * CORES
PICKS = ((0, 0, 1, 1), (1, 1, 0, 0))
F32 = jnp.float32


def join(left, right):
    la, lb, lc, lg, lh = left
    ra, rb, rc, rg, rh = right
    inv = 1.0 / (lc + ra)
    left_share = lb * inv
    right_share = rb * inv
    gap = lh - rg
    merged = (
        la - lb * left_share,
        lb * right_share,
        rc - rb * right_share,
        lg - left_share * gap,
        rh + right_share * gap,
    )
    return merged, (inv * gap, left_share, right_share)


def join_all(pieces):
    if len(pieces) == 1:
        return pieces[0], None
    half = len(pieces) // 2
    left, left_tree = join_all(pieces[:half])
    right, right_tree = join_all(pieces[half:])
    merged, face = join(left, right)
    return merged, (face, left_tree, right_tree)


def face_fluxes(tree, low, high):
    if tree is None:
        return [low, high]
    face, left_tree, right_tree = tree
    flux = face[0]
    if low is not None:
        flux = flux + face[1] * low
    if high is not None:
        flux = flux + face[2] * high
    return face_fluxes(left_tree, low, flux) + face_fluxes(right_tree, flux, high)[1:]


def tree_shape(count):
    if count == 1:
        return None
    return (count, tree_shape(count // 2), tree_shape(count // 2))


def tree_values(tree):
    if tree is None:
        return []
    return list(tree[0]) + tree_values(tree[1]) + tree_values(tree[2])


def tree_of(shape, values):
    if shape is None:
        return None
    face = tuple(values.pop(0) for _ in range(3))
    left = tree_of(shape[1], values)
    return (face, left, tree_of(shape[2], values))


def plane(ref, i, rows):
    return ref[i * rows : (i + 1) * rows, :]


def eliminate(ratio, half, count):
    gaps = [half[i] + half[i + 1] for i in range(count - 1)]
    up = []
    total = ratio[0]
    for i in range(count - 1):
        carry = 1.0 / (1.0 + total * gaps[i])
        up.append(carry)
        total = ratio[i + 1] + total * carry
    last_inv = 1.0 / total
    down = [None] * (count - 1)
    total = ratio[count - 1]
    for i in range(count - 2, -1, -1):
        carry = 1.0 / (1.0 + total * gaps[i])
        down[i] = carry
        total = ratio[i] + total * carry
    first_inv = 1.0 / total
    across = last_inv
    for i in range(count - 2, -1, -1):
        across = across * up[i]
    ends = [first_inv + half[0], across, last_inv + half[count - 1], first_inv, last_inv]
    return gaps, up, down, ends


def offsets(right, up, down, first_inv, last_inv, count):
    rising = right[0]
    for i in range(count - 1):
        rising = right[i + 1] + up[i] * rising
    falling = right[count - 1]
    for i in range(count - 2, -1, -1):
        falling = right[i] + down[i] * falling
    return falling * first_inv, rising * last_inv


def substitute(right, gaps, up, last_inv, low, high, count):
    sums = [right[0] + low]
    for i in range(count - 1):
        sums.append(right[i + 1] + up[i] * sums[i])
    values = [None] * count
    values[count - 1] = (sums[count - 1] - high) * last_inv
    for i in range(count - 2, -1, -1):
        values[i] = up[i] * (values[i + 1] + gaps[i] * sums[i])
    return values


def local_step(sizes, sizes_mesh, pressure, source, porosity, permeability, speed):
    nx, ny, nz = sizes
    count_gx, count_gy = sizes_mesh
    far_x = count_gx // NEAR_X
    far_y = count_gy // NEAR_Y
    near_x_groups = [[z * NEAR_X + x for x in range(NEAR_X)] for z in range(far_x)]
    far_x_groups = [
        [k * NEAR_X + pick[k] * RING_X + x for k in range(far_x)] for pick in PICKS for x in range(RING_X)
    ]
    near_y_groups = [[y * NEAR_Y + c for c in range(NEAR_Y)] for y in range(far_y)]
    chip_groups = [[y + c for c in range(CORES)] for y in range(0, count_gy, CORES)]
    far_y_groups = [
        [k * NEAR_Y + pick[k] * CORES + c for k in range(far_y)] for pick in PICKS for c in range(CORES)
    ]
    cells = nx * ny
    pressure = pressure.reshape(cells, nz)
    source = source.reshape(cells, nz)
    porosity = porosity.reshape(cells, nz)
    permeability = permeability.reshape(cells, nz)
    speed = speed.reshape(cells, nz)

    def call(body, shapes, scratch, *args, name):
        return pl.pallas_call(
            body,
            out_shape=[jax.ShapeDtypeStruct(s, F32) for s in shapes],
            in_specs=[pl.BlockSpec(memory_space=pltpu.VMEM)] * len(args),
            out_specs=[pl.BlockSpec(memory_space=pltpu.VMEM)] * len(shapes),
            scratch_shapes=[pltpu.VMEM(s, F32) for s in scratch],
            compiler_params=pltpu.CompilerParams(vmem_limit_bytes=32 * 1024 * 1024),
            name=name,
        )(*args)

    def rows_y(ref, j):
        return ref[pl.ds(j, nx, stride=ny), :]

    def halves_body(
        p_hbm, source_hbm, por_hbm, perm_hbm, speed_hbm,
        half_ref, near_ref, far_ref, p_ref, source_ref, por_ref, perm_ref, speed_ref, sems,
    ):
        pairs = (
            (perm_hbm, perm_ref), (speed_hbm, speed_ref), (p_hbm, p_ref),
            (source_hbm, source_ref), (por_hbm, por_ref),
        )
        copies = [pltpu.make_async_copy(a, b, sems.at[n]) for n, (a, b) in enumerate(pairs)]
        for copy in copies:
            copy.start()
        for copy in copies[:3]:
            copy.wait()
        for i in range(nx):
            root = lax.rsqrt(plane(perm_ref, i, ny).astype(F32))
            half_ref[i * ny : (i + 1) * ny, :] = (0.5 * root) * (
                root + FORCH * plane(speed_ref, i, ny).astype(F32)
            )
        even = lax.rem(lax.axis_index("gy"), 2) == 0
        for k, ref in enumerate((half_ref, p_ref)):
            low = rows_y(ref, 0)
            high = rows_y(ref, ny - 1)
            near_ref[k] = jnp.where(even, high, low)
            far_ref[k] = jnp.where(even, low, high)
        for copy in copies[3:]:
            copy.wait()

    vmem = pl.BlockSpec(memory_space=pltpu.VMEM)
    half, near_send, far_send, pressure, source, porosity = pl.pallas_call(
        halves_body,
        out_shape=[
            jax.ShapeDtypeStruct((cells, nz), F32),
            jax.ShapeDtypeStruct((2, nx, nz), F32),
            jax.ShapeDtypeStruct((2, nx, nz), F32),
            jax.ShapeDtypeStruct((cells, nz), F32),
            jax.ShapeDtypeStruct((cells, nz), F32),
            jax.ShapeDtypeStruct((cells, nz), porosity.dtype),
        ],
        in_specs=[pl.BlockSpec(memory_space=pltpu.HBM)] * 5,
        out_specs=[vmem] * 6,
        scratch_shapes=[
            pltpu.VMEM((cells, nz), permeability.dtype),
            pltpu.VMEM((cells, nz), speed.dtype),
            pltpu.SemaphoreType.DMA((5,)),
        ],
        compiler_params=pltpu.CompilerParams(vmem_limit_bytes=16 * 1024 * 1024),
        name="halves",
    )(*(pltpu.with_memory_space_constraint(a, pltpu.HBM) for a in (pressure, source, porosity, permeability, speed)))
    far_pairs = []
    for i in range(1, count_gy - 1, 2):
        far_pairs += [(i, i + 1), (i + 1, i)]
    far_got = lax.ppermute(far_send, "gy", far_pairs)
    near_got = lax.all_gather(near_send, "gy", axis=0, axis_index_groups=chip_groups)

    def inner_body(
        p_ref, source_ref, por_ref, half_ref,
        right_ref, ratio_ref, xup_ref, xdown_ref, xends_ref, yup_ref, ydown_ref, yends_ref,
    ):
        lane = lax.broadcasted_iota(jnp.int32, (ny, nz), 1)
        row = lax.broadcasted_iota(jnp.int32, (ny, nz), 0)
        for i in range(nx):
            p = plane(p_ref, i, ny)
            h = plane(half_ref, i, ny)
            ratio = plane(por_ref, i, ny).astype(F32) * (1.0 / STEP)
            ratio_ref[i * ny : (i + 1) * ny, :] = ratio
            flux_z = (pltpu.roll(p, nz - 1, 1) - p) / (pltpu.roll(h, nz - 1, 1) + h)
            flux_z = jnp.where(lane == nz - 1, 0.0, flux_z)
            flux_y = (pltpu.roll(p, ny - 1, 0) - p) / (pltpu.roll(h, ny - 1, 0) + h)
            flux_y = jnp.where(row == ny - 1, 0.0, flux_y)
            lap = (flux_z - pltpu.roll(flux_z, 1, 1)) + (flux_y - pltpu.roll(flux_y, 1, 0))
            right_ref[i * ny : (i + 1) * ny, :] = (lap - plane(source_ref, i, ny)) + ratio * p
        ratios = [plane(ratio_ref, i, ny) for i in range(nx)]
        halves = [plane(half_ref, i, ny) for i in range(nx)]
        _, up, down, ends = eliminate(ratios, halves, nx)
        for i in range(nx - 1):
            xup_ref[i] = up[i]
            xdown_ref[i] = down[i]
        for k in range(5):
            xends_ref[k] = ends[k]
        ratios = [rows_y(ratio_ref, j) for j in range(ny)]
        halves = [rows_y(half_ref, j) for j in range(ny)]
        _, up, down, ends = eliminate(ratios, halves, ny)
        for j in range(ny - 1):
            yup_ref[j] = up[j]
            ydown_ref[j] = down[j]
        for k in range(5):
            yends_ref[k] = ends[k]

    right0, ratio, xup, xdown, xends, yup, ydown, yends = call(
        inner_body,
        [
            (cells, nz), (cells, nz), (nx - 1, ny, nz), (nx - 1, ny, nz), (5, ny, nz),
            (ny - 1, nx, nz), (ny - 1, nx, nz), (5, nx, nz),
        ],
        [], pressure, source, porosity, half, name="inner",
    )

    def edges_body(
        right0_ref, p_ref, half_ref, far_ref, near_ref, xup_ref, xdown_ref, xends_ref, right_ref, send_ref
    ):
        place = lax.axis_index("gy")
        even = lax.rem(place, 2) == 0
        right_ref[...] = right0_ref[...]
        for j, is_end, low in ((0, place == 0, True), (ny - 1, place == count_gy - 1, False)):
            other_h, other_p = (
                jnp.where(even, far_ref[k], near_ref[0, k]) if low else jnp.where(even, near_ref[1, k], far_ref[k])
                for k in range(2)
            )
            flux = (other_p - rows_y(p_ref, j)) / (other_h + rows_y(half_ref, j))
            flux = jnp.where(is_end, 0.0, flux)
            right_ref[pl.ds(j, nx, stride=ny), :] = rows_y(right_ref, j) + flux
        right = [plane(right_ref, i, ny) for i in range(nx)]
        up = [xup_ref[i] for i in range(nx - 1)]
        down = [xdown_ref[i] for i in range(nx - 1)]
        first, last = offsets(right, up, down, xends_ref[3], xends_ref[4], nx)
        for k, value in enumerate((xends_ref[0], xends_ref[1], xends_ref[2], first, last)):
            for target in range(NEAR_X):
                send_ref[target, k] = value

    right, near_x = call(
        edges_body, [(cells, nz), (NEAR_X, 5, ny, nz)], [],
        right0, pressure, half, far_got, near_got, xup, xdown, xends, name="edges",
    )
    near_x = lax.all_to_all(near_x, "gx", 0, 0, axis_index_groups=near_x_groups)

    def ring_body(got_ref, send_ref, tree_ref):
        pieces = [tuple(got_ref[n, k] for k in range(5)) for n in range(NEAR_X)]
        merged, tree = join_all(pieces)
        for k in range(5):
            for target in range(far_x):
                send_ref[target, k] = merged[k]
        for k, value in enumerate(tree_values(tree)):
            tree_ref[k] = value

    far_x_send, x_tree = call(
        ring_body, [(far_x, 5, ny, nz), (3 * (NEAR_X - 1), ny, nz)], [], near_x, name="x_ring"
    )
    far_x_got = lax.all_to_all(far_x_send, "gx", 0, 0, axis_index_groups=far_x_groups)

    def along_x_body(
        got_ref, tree_ref, right_ref, half_ref, ratio_ref, p_ref, xup_ref, xends_ref,
        yup_ref, ydown_ref, yends_ref,
        send_ref, yright_ref, far_faces, near_faces, solved_ref,
    ):
        place = lax.axis_index("gx")
        far = place // NEAR_X
        near = lax.rem(place, NEAR_X)
        pieces = [tuple(got_ref[n, k] for k in range(5)) for n in range(far_x)]
        _, tree = join_all(pieces)
        fluxes = face_fluxes(tree, None, None)
        zero = jnp.zeros((ny, nz), F32)
        for k, value in enumerate(fluxes):
            far_faces[k] = zero if value is None else value
        low = far_faces[far]
        high = far_faces[far + 1]
        tree = tree_of(tree_shape(NEAR_X), [tree_ref[k] for k in range(3 * (NEAR_X - 1))])
        for k, value in enumerate(face_fluxes(tree, low, high)):
            near_faces[k] = value
        low = near_faces[near]
        high = near_faces[near + 1]
        gaps = [plane(half_ref, i, ny) + plane(half_ref, i + 1, ny) for i in range(nx - 1)]
        up = [xup_ref[i] for i in range(nx - 1)]
        right = [plane(right_ref, i, ny) for i in range(nx)]
        values = substitute(right, gaps, up, xends_ref[4], low, high, nx)
        for i in range(nx):
            solved_ref[i * ny : (i + 1) * ny, :] = plane(ratio_ref, i, ny) * (values[i] - plane(p_ref, i, ny))
        yright = [rows_y(solved_ref, j) for j in range(ny)]
        for j in range(ny):
            yright_ref[j] = yright[j]
        up = [yup_ref[j] for j in range(ny - 1)]
        down = [ydown_ref[j] for j in range(ny - 1)]
        first, last = offsets(yright, up, down, yends_ref[3], yends_ref[4], ny)
        for k, value in enumerate((yends_ref[0], yends_ref[1], yends_ref[2], first, last)):
            send_ref[k] = value

    pair_send, yright = call(
        along_x_body,
        [(5, nx, nz), (ny, nx, nz)],
        [(far_x + 1, ny, nz), (NEAR_X + 1, ny, nz), (cells, nz)],
        far_x_got, x_tree, right, half, ratio, pressure, xup, xends, yup, ydown, yends,
        name="along_x",
    )
    pair_got = lax.all_gather(pair_send, "gy", axis=0, axis_index_groups=near_y_groups)

    def pair_body(got_ref, send_ref, tree_ref):
        pieces = [tuple(got_ref[n, k] for k in range(5)) for n in range(NEAR_Y)]
        merged, tree = join_all(pieces)
        for k in range(5):
            for target in range(far_y):
                send_ref[target, k] = merged[k]
        for k, value in enumerate(tree_values(tree)):
            tree_ref[k] = value

    far_y_send, y_tree = call(
        pair_body, [(far_y, 5, nx, nz), (3 * (NEAR_Y - 1), nx, nz)], [], pair_got, name="y_pair"
    )
    far_y_got = lax.all_to_all(far_y_send, "gy", 0, 0, axis_index_groups=far_y_groups)

    def updated_body(
        got_ref, tree_ref, yright_ref, half_ref, p_ref, yup_ref, yends_ref, out_ref, far_faces, near_faces
    ):
        place = lax.axis_index("gy")
        far = place // NEAR_Y
        near = lax.rem(place, NEAR_Y)
        pieces = [tuple(got_ref[n, k] for k in range(5)) for n in range(far_y)]
        _, tree = join_all(pieces)
        zero = jnp.zeros((nx, nz), F32)
        for k, value in enumerate(face_fluxes(tree, None, None)):
            far_faces[k] = zero if value is None else value
        low = far_faces[far]
        high = far_faces[far + 1]
        tree = tree_of(tree_shape(NEAR_Y), [tree_ref[k] for k in range(3 * (NEAR_Y - 1))])
        for k, value in enumerate(face_fluxes(tree, low, high)):
            near_faces[k] = value
        low = near_faces[near]
        high = near_faces[near + 1]
        halves = [rows_y(half_ref, j) for j in range(ny)]
        gaps = [halves[j] + halves[j + 1] for j in range(ny - 1)]
        up = [yup_ref[j] for j in range(ny - 1)]
        right = [yright_ref[j] for j in range(ny)]
        values = substitute(right, gaps, up, yends_ref[4], low, high, ny)
        for j in range(ny):
            out_ref[pl.ds(j, nx, stride=ny), :] = rows_y(p_ref, j) + values[j]

    (updated,) = call(
        updated_body,
        [(cells, nz)],
        [(far_y + 1, nx, nz), (NEAR_Y + 1, nx, nz)],
        far_y_got, y_tree, yright, half, pressure, yup, yends,
        name="updated",
    )
    return updated.reshape(nx, ny, nz)


def solution(mesh):
    spec = P("gx", "gy", None)
    sizes_mesh = (mesh.shape["gx"], mesh.shape["gy"])

    def local(pressure, source, porosity, permeability, speed):
        return local_step(
            pressure.shape, sizes_mesh, pressure, source, porosity, permeability, speed
        )

    return jax.shard_map(
        local, mesh=mesh, in_specs=(spec,) * 5, out_specs=spec, check_vma=False
    )
```

```python
import jax
import jax.numpy as jnp
from jax import lax
from jax.experimental import pallas as pl
from jax.experimental.pallas import tpu as pltpu
from jax.sharding import PartitionSpec as P

FORCH = 0.55
STEP = 500.0
RING_X = 4
CORES = 2
NEAR_X = 2 * RING_X
NEAR_Y = 2 * CORES
PICKS = ((0, 0, 1, 1), (1, 1, 0, 0))
F32 = jnp.float32


def join(left, right):
    la, lb, lc, lg, lh = left
    ra, rb, rc, rg, rh = right
    inv = 1.0 / (lc + ra)
    left_share = lb * inv
    right_share = rb * inv
    gap = lh - rg
    merged = (
        la - lb * left_share,
        lb * right_share,
        rc - rb * right_share,
        lg - left_share * gap,
        rh + right_share * gap,
    )
    return merged, (inv * gap, left_share, right_share)


def join_all(pieces):
    if len(pieces) == 1:
        return pieces[0], None
    half = len(pieces) // 2
    left, left_tree = join_all(pieces[:half])
    right, right_tree = join_all(pieces[half:])
    merged, face = join(left, right)
    return merged, (face, left_tree, right_tree)


def face_fluxes(tree, low, high):
    if tree is None:
        return [low, high]
    face, left_tree, right_tree = tree
    flux = face[0]
    if low is not None:
        flux = flux + face[1] * low
    if high is not None:
        flux = flux + face[2] * high
    return face_fluxes(left_tree, low, flux) + face_fluxes(right_tree, flux, high)[1:]


def tree_shape(count):
    if count == 1:
        return None
    return (count, tree_shape(count // 2), tree_shape(count // 2))


def tree_values(tree):
    if tree is None:
        return []
    return list(tree[0]) + tree_values(tree[1]) + tree_values(tree[2])


def tree_of(shape, values):
    if shape is None:
        return None
    face = tuple(values.pop(0) for _ in range(3))
    left = tree_of(shape[1], values)
    return (face, left, tree_of(shape[2], values))


def plane(ref, i, rows):
    return ref[i * rows : (i + 1) * rows, :]


def elimination(ratio, half, count, keep):
    gaps = [half(i) + half(i + 1) for i in range(count - 1)]
    rising = ratio(0)
    falling = ratio(count - 1)
    through = None
    for i in range(count - 1):
        up = 1.0 / (1.0 + rising * gaps[i])
        rising = ratio(i + 1) + rising * up
        through = up if through is None else through * up
        k = count - 2 - i
        down = 1.0 / (1.0 + falling * gaps[k])
        falling = ratio(k) + falling * down
        keep(i, up, through, k, down)
        yield None
    last_inv = 1.0 / rising
    first_inv = 1.0 / falling
    yield (first_inv + half(0), through * last_inv, last_inv + half(count - 1), first_inv, last_inv)


def interleave(*parts):
    last = [None] * len(parts)
    running = list(range(len(parts)))
    while running:
        for n in list(running):
            try:
                last[n] = next(parts[n])
            except StopIteration:
                running.remove(n)
    return last


def offsets(right, up, down, first_inv, last_inv, count):
    rising = right[0]
    falling = right[count - 1]
    sums = [rising]
    for i in range(count - 1):
        rising = right[i + 1] + up[i] * rising
        sums.append(rising)
        k = count - 2 - i
        falling = right[k] + down[k] * falling
    return falling * first_inv, rising * last_inv, sums


def substitute(sums, through, gaps, up, last_inv, low, high, count):
    values = [None] * count
    values[count - 1] = ((sums[count - 1] + through[count - 2] * low) - high) * last_inv
    for i in range(count - 2, -1, -1):
        inner = low if i == 0 else through[i - 1] * low
        values[i] = up[i] * (values[i + 1] + gaps[i] * (sums[i] + inner))
    return values


def local_step(sizes, sizes_mesh, pressure, source, porosity, permeability, speed):
    nx, ny, nz = sizes
    count_gx, count_gy = sizes_mesh
    far_x = count_gx // NEAR_X
    far_y = count_gy // NEAR_Y
    near_x_groups = [[z * NEAR_X + x for x in range(NEAR_X)] for z in range(far_x)]
    far_x_groups = [
        [k * NEAR_X + pick[k] * RING_X + x for k in range(far_x)] for pick in PICKS for x in range(RING_X)
    ]
    near_y_groups = [[y * NEAR_Y + c for c in range(NEAR_Y)] for y in range(far_y)]
    chip_groups = [[y + c for c in range(CORES)] for y in range(0, count_gy, CORES)]
    far_y_groups = [
        [k * NEAR_Y + pick[k] * CORES + c for k in range(far_y)] for pick in PICKS for c in range(CORES)
    ]
    cells = nx * ny
    pressure = pressure.reshape(cells, nz)
    source = source.reshape(cells, nz)
    porosity = porosity.reshape(cells, nz)
    permeability = permeability.reshape(cells, nz)
    speed = speed.reshape(cells, nz)

    def call(body, shapes, scratch, *args, name):
        return pl.pallas_call(
            body,
            out_shape=[jax.ShapeDtypeStruct(s, F32) for s in shapes],
            in_specs=[pl.BlockSpec(memory_space=pltpu.VMEM)] * len(args),
            out_specs=[pl.BlockSpec(memory_space=pltpu.VMEM)] * len(shapes),
            scratch_shapes=[pltpu.VMEM(s, F32) for s in scratch],
            compiler_params=pltpu.CompilerParams(vmem_limit_bytes=32 * 1024 * 1024),
            name=name,
        )(*args)

    def rows_y(ref, j):
        return ref[pl.ds(j, nx, stride=ny), :]

    def halves_body(
        p_hbm, source_hbm, por_hbm, perm_hbm, speed_hbm,
        half_ref, near_ref, far_ref, p_ref, source_ref, por_ref, perm_ref, speed_ref, sems,
    ):
        pairs = (
            (perm_hbm, perm_ref), (speed_hbm, speed_ref), (p_hbm, p_ref),
            (source_hbm, source_ref), (por_hbm, por_ref),
        )
        copies = [pltpu.make_async_copy(a, b, sems.at[n]) for n, (a, b) in enumerate(pairs)]
        for copy in copies:
            copy.start()
        for copy in copies[:3]:
            copy.wait()
        for i in range(nx):
            root = lax.rsqrt(plane(perm_ref, i, ny).astype(F32))
            half_ref[i * ny : (i + 1) * ny, :] = (0.5 * root) * (
                root + FORCH * plane(speed_ref, i, ny).astype(F32)
            )
        even = lax.rem(lax.axis_index("gy"), 2) == 0
        for k, ref in enumerate((half_ref, p_ref)):
            low = rows_y(ref, 0)
            high = rows_y(ref, ny - 1)
            near_ref[k] = jnp.where(even, high, low)
            far_ref[k] = jnp.where(even, low, high)
        for copy in copies[3:]:
            copy.wait()

    vmem = pl.BlockSpec(memory_space=pltpu.VMEM)
    half, near_send, far_send, pressure, source, porosity = pl.pallas_call(
        halves_body,
        out_shape=[
            jax.ShapeDtypeStruct((cells, nz), F32),
            jax.ShapeDtypeStruct((2, nx, nz), F32),
            jax.ShapeDtypeStruct((2, nx, nz), F32),
            jax.ShapeDtypeStruct((cells, nz), F32),
            jax.ShapeDtypeStruct((cells, nz), F32),
            jax.ShapeDtypeStruct((cells, nz), porosity.dtype),
        ],
        in_specs=[pl.BlockSpec(memory_space=pltpu.HBM)] * 5,
        out_specs=[vmem] * 6,
        scratch_shapes=[
            pltpu.VMEM((cells, nz), permeability.dtype),
            pltpu.VMEM((cells, nz), speed.dtype),
            pltpu.SemaphoreType.DMA((5,)),
        ],
        compiler_params=pltpu.CompilerParams(vmem_limit_bytes=16 * 1024 * 1024),
        name="halves",
    )(*(pltpu.with_memory_space_constraint(a, pltpu.HBM) for a in (pressure, source, porosity, permeability, speed)))
    far_pairs = []
    for i in range(1, count_gy - 1, 2):
        far_pairs += [(i, i + 1), (i + 1, i)]
    far_got = lax.ppermute(far_send, "gy", far_pairs)
    near_got = lax.all_gather(near_send, "gy", axis=0, axis_index_groups=chip_groups)

    def inner_body(
        p_ref, source_ref, por_ref, half_ref,
        right_ref, ratio_ref, xup_ref, xthrough_ref, xdown_ref, xends_ref,
        yup_ref, ythrough_ref, ydown_ref, yends_ref,
    ):
        lane = lax.broadcasted_iota(jnp.int32, (ny, nz), 1)
        row = lax.broadcasted_iota(jnp.int32, (ny, nz), 0)
        for i in range(nx):
            ratio_ref[i * ny : (i + 1) * ny, :] = plane(por_ref, i, ny).astype(F32) * (1.0 / STEP)

        def right_side():
            for i in range(nx):
                p = plane(p_ref, i, ny)
                h = plane(half_ref, i, ny)
                flux_z = (pltpu.roll(p, nz - 1, 1) - p) / (pltpu.roll(h, nz - 1, 1) + h)
                flux_z = jnp.where(lane == nz - 1, 0.0, flux_z)
                flux_y = (pltpu.roll(p, ny - 1, 0) - p) / (pltpu.roll(h, ny - 1, 0) + h)
                flux_y = jnp.where(row == ny - 1, 0.0, flux_y)
                lap = (flux_z - pltpu.roll(flux_z, 1, 1)) + (flux_y - pltpu.roll(flux_y, 1, 0))
                right_ref[i * ny : (i + 1) * ny, :] = (lap - plane(source_ref, i, ny)) + plane(ratio_ref, i, ny) * p
                yield None

        def keep_x(i, up, through, k, down):
            xup_ref[i] = up
            xthrough_ref[i] = through
            xdown_ref[k] = down

        def keep_y(i, up, through, k, down):
            yup_ref[i] = up
            ythrough_ref[i] = through
            ydown_ref[k] = down

        xends, yends, _ = interleave(
            elimination(lambda i: plane(ratio_ref, i, ny), lambda i: plane(half_ref, i, ny), nx, keep_x),
            elimination(lambda j: rows_y(ratio_ref, j), lambda j: rows_y(half_ref, j), ny, keep_y),
            right_side(),
        )
        for k in range(5):
            xends_ref[k] = xends[k]
            yends_ref[k] = yends[k]

    right0, ratio, xup, xthrough, xdown, xends, yup, ythrough, ydown, yends = call(
        inner_body,
        [
            (cells, nz), (cells, nz), (nx - 1, ny, nz), (nx - 1, ny, nz), (nx - 1, ny, nz), (5, ny, nz),
            (ny - 1, nx, nz), (ny - 1, nx, nz), (ny - 1, nx, nz), (5, nx, nz),
        ],
        [], pressure, source, porosity, half, name="inner",
    )

    def edges_body(
        right0_ref, p_ref, half_ref, far_ref, near_ref, xup_ref, xdown_ref, xends_ref, sums_ref, send_ref, right_ref
    ):
        place = lax.axis_index("gy")
        even = lax.rem(place, 2) == 0
        right_ref[...] = right0_ref[...]
        for j, is_end, low in ((0, place == 0, True), (ny - 1, place == count_gy - 1, False)):
            other_h, other_p = (
                jnp.where(even, far_ref[k], near_ref[0, k]) if low else jnp.where(even, near_ref[1, k], far_ref[k])
                for k in range(2)
            )
            flux = (other_p - rows_y(p_ref, j)) / (other_h + rows_y(half_ref, j))
            flux = jnp.where(is_end, 0.0, flux)
            right_ref[pl.ds(j, nx, stride=ny), :] = rows_y(right_ref, j) + flux
        right = [plane(right_ref, i, ny) for i in range(nx)]
        up = [xup_ref[i] for i in range(nx - 1)]
        down = [xdown_ref[i] for i in range(nx - 1)]
        first, last, sums = offsets(right, up, down, xends_ref[3], xends_ref[4], nx)
        for i in range(nx):
            sums_ref[i] = sums[i]
        for k, value in enumerate((xends_ref[0], xends_ref[1], xends_ref[2], first, last)):
            for target in range(NEAR_X):
                send_ref[target, k] = value

    xsums, near_x = call(
        edges_body, [(nx, ny, nz), (NEAR_X, 5, ny, nz)], [(cells, nz)],
        right0, pressure, half, far_got, near_got, xup, xdown, xends, name="edges",
    )
    near_x = lax.all_to_all(near_x, "gx", 0, 0, axis_index_groups=near_x_groups)

    def ring_body(got_ref, send_ref, tree_ref):
        pieces = [tuple(got_ref[n, k] for k in range(5)) for n in range(NEAR_X)]
        merged, tree = join_all(pieces)
        for k in range(5):
            for target in range(far_x):
                send_ref[target, k] = merged[k]
        for k, value in enumerate(tree_values(tree)):
            tree_ref[k] = value

    far_x_send, x_tree = call(
        ring_body, [(far_x, 5, ny, nz), (3 * (NEAR_X - 1), ny, nz)], [], near_x, name="x_ring"
    )
    far_x_got = lax.all_to_all(far_x_send, "gx", 0, 0, axis_index_groups=far_x_groups)

    def along_x_body(
        got_ref, tree_ref, xsums_ref, half_ref, ratio_ref, p_ref, xup_ref, xthrough_ref, xends_ref,
        yup_ref, ydown_ref, yends_ref,
        send_ref, ysums_ref, far_faces, near_faces, solved_ref,
    ):
        place = lax.axis_index("gx")
        far = place // NEAR_X
        near = lax.rem(place, NEAR_X)
        pieces = [tuple(got_ref[n, k] for k in range(5)) for n in range(far_x)]
        _, tree = join_all(pieces)
        fluxes = face_fluxes(tree, None, None)
        zero = jnp.zeros((ny, nz), F32)
        for k, value in enumerate(fluxes):
            far_faces[k] = zero if value is None else value
        low = far_faces[far]
        high = far_faces[far + 1]
        tree = tree_of(tree_shape(NEAR_X), [tree_ref[k] for k in range(3 * (NEAR_X - 1))])
        for k, value in enumerate(face_fluxes(tree, low, high)):
            near_faces[k] = value
        low = near_faces[near]
        high = near_faces[near + 1]
        gaps = [plane(half_ref, i, ny) + plane(half_ref, i + 1, ny) for i in range(nx - 1)]
        up = [xup_ref[i] for i in range(nx - 1)]
        through = [xthrough_ref[i] for i in range(nx - 1)]
        sums = [xsums_ref[i] for i in range(nx)]
        values = substitute(sums, through, gaps, up, xends_ref[4], low, high, nx)
        for i in range(nx):
            solved_ref[i * ny : (i + 1) * ny, :] = plane(ratio_ref, i, ny) * (values[i] - plane(p_ref, i, ny))
        yright = [rows_y(solved_ref, j) for j in range(ny)]
        up = [yup_ref[j] for j in range(ny - 1)]
        down = [ydown_ref[j] for j in range(ny - 1)]
        first, last, sums = offsets(yright, up, down, yends_ref[3], yends_ref[4], ny)
        for j in range(ny):
            ysums_ref[j] = sums[j]
        for k, value in enumerate((yends_ref[0], yends_ref[1], yends_ref[2], first, last)):
            send_ref[k] = value

    pair_send, ysums = call(
        along_x_body,
        [(5, nx, nz), (ny, nx, nz)],
        [(far_x + 1, ny, nz), (NEAR_X + 1, ny, nz), (cells, nz)],
        far_x_got, x_tree, xsums, half, ratio, pressure, xup, xthrough, xends, yup, ydown, yends,
        name="along_x",
    )
    pair_got = lax.all_gather(pair_send, "gy", axis=0, axis_index_groups=near_y_groups)

    def pair_body(got_ref, send_ref, tree_ref):
        pieces = [tuple(got_ref[n, k] for k in range(5)) for n in range(NEAR_Y)]
        merged, tree = join_all(pieces)
        for k in range(5):
            for target in range(far_y):
                send_ref[target, k] = merged[k]
        for k, value in enumerate(tree_values(tree)):
            tree_ref[k] = value

    far_y_send, y_tree = call(
        pair_body, [(far_y, 5, nx, nz), (3 * (NEAR_Y - 1), nx, nz)], [], pair_got, name="y_pair"
    )
    far_y_got = lax.all_to_all(far_y_send, "gy", 0, 0, axis_index_groups=far_y_groups)

    def updated_body(
        got_ref, tree_ref, ysums_ref, half_ref, p_ref, yup_ref, ythrough_ref, yends_ref, out_ref, far_faces, near_faces
    ):
        place = lax.axis_index("gy")
        far = place // NEAR_Y
        near = lax.rem(place, NEAR_Y)
        pieces = [tuple(got_ref[n, k] for k in range(5)) for n in range(far_y)]
        _, tree = join_all(pieces)
        zero = jnp.zeros((nx, nz), F32)
        for k, value in enumerate(face_fluxes(tree, None, None)):
            far_faces[k] = zero if value is None else value
        low = far_faces[far]
        high = far_faces[far + 1]
        tree = tree_of(tree_shape(NEAR_Y), [tree_ref[k] for k in range(3 * (NEAR_Y - 1))])
        for k, value in enumerate(face_fluxes(tree, low, high)):
            near_faces[k] = value
        low = near_faces[near]
        high = near_faces[near + 1]
        halves = [rows_y(half_ref, j) for j in range(ny)]
        gaps = [halves[j] + halves[j + 1] for j in range(ny - 1)]
        up = [yup_ref[j] for j in range(ny - 1)]
        through = [ythrough_ref[j] for j in range(ny - 1)]
        sums = [ysums_ref[j] for j in range(ny)]
        values = substitute(sums, through, gaps, up, yends_ref[4], low, high, ny)
        for j in range(ny):
            out_ref[pl.ds(j, nx, stride=ny), :] = rows_y(p_ref, j) + values[j]

    (updated,) = call(
        updated_body,
        [(cells, nz)],
        [(far_y + 1, nx, nz), (NEAR_Y + 1, nx, nz)],
        far_y_got, y_tree, ysums, half, pressure, yup, ythrough, yends,
        name="updated",
    )
    return updated.reshape(nx, ny, nz)


def solution(mesh):
    spec = P("gx", "gy", None)
    sizes_mesh = (mesh.shape["gx"], mesh.shape["gy"])

    def local(pressure, source, porosity, permeability, speed):
        return local_step(
            pressure.shape, sizes_mesh, pressure, source, porosity, permeability, speed
        )

    return jax.shard_map(
        local, mesh=mesh, in_specs=(spec,) * 5, out_specs=spec, check_vma=False
    )
```

```python
import jax
import jax.numpy as jnp
from jax import lax
from jax.experimental import pallas as pl
from jax.experimental.pallas import tpu as pltpu
from jax.sharding import PartitionSpec as P

FORCH = 0.55
STEP = 500.0
RING_X = 4
CORES = 2
NEAR_X = 2 * RING_X
NEAR_Y = 2 * CORES
PICKS = ((0, 0, 1, 1), (1, 1, 0, 0))
F32 = jnp.float32
NEAR_X_ORDER = (7, 6, 5, 4, 3, 2, 1, 0)
FAR_X_ORDER = (3, 2, 1, 0)
FAR_Y_ORDER = (2, 3, 1, 0)


def join(left, right):
    la, lb, lc, lg, lh = left
    ra, rb, rc, rg, rh = right
    inv = 1.0 / (lc + ra)
    left_share = lb * inv
    right_share = rb * inv
    gap = lh - rg
    merged = (
        la - lb * left_share,
        lb * right_share,
        rc - rb * right_share,
        lg - left_share * gap,
        rh + right_share * gap,
    )
    return merged, (inv * gap, left_share, right_share)


def join_all(pieces):
    if len(pieces) == 1:
        return pieces[0], None
    half = len(pieces) // 2
    left, left_tree = join_all(pieces[:half])
    right, right_tree = join_all(pieces[half:])
    merged, face = join(left, right)
    return merged, (face, left_tree, right_tree)


def face_fluxes(tree, low, high):
    if tree is None:
        return [low, high]
    face, left_tree, right_tree = tree
    flux = face[0]
    if low is not None:
        flux = flux + face[1] * low
    if high is not None:
        flux = flux + face[2] * high
    return face_fluxes(left_tree, low, flux) + face_fluxes(right_tree, flux, high)[1:]


def tree_shape(count):
    if count == 1:
        return None
    return (count, tree_shape(count // 2), tree_shape(count // 2))


def tree_values(tree):
    if tree is None:
        return []
    return list(tree[0]) + tree_values(tree[1]) + tree_values(tree[2])


def tree_of(shape, values):
    if shape is None:
        return None
    face = tuple(values.pop(0) for _ in range(3))
    left = tree_of(shape[1], values)
    return (face, left, tree_of(shape[2], values))


def plane(ref, i, rows):
    return ref[i * rows : (i + 1) * rows, :]


def elimination(ratio, half, count, keep):
    gaps = [half(i) + half(i + 1) for i in range(count - 1)]
    rising = ratio(0)
    falling = ratio(count - 1)
    through = None
    for i in range(count - 1):
        up = 1.0 / (1.0 + rising * gaps[i])
        rising = ratio(i + 1) + rising * up
        through = up if through is None else through * up
        k = count - 2 - i
        down = 1.0 / (1.0 + falling * gaps[k])
        falling = ratio(k) + falling * down
        keep(i, up, through, k, down)
        yield None
    last_inv = 1.0 / rising
    first_inv = 1.0 / falling
    yield (first_inv + half(0), through * last_inv, last_inv + half(count - 1), first_inv, last_inv)


def interleave(*parts):
    last = [None] * len(parts)
    running = list(range(len(parts)))
    while running:
        for n in list(running):
            try:
                last[n] = next(parts[n])
            except StopIteration:
                running.remove(n)
    return last


def offsets(right, up, down, first_inv, last_inv, count):
    rising = right[0]
    falling = right[count - 1]
    sums = [rising]
    for i in range(count - 1):
        rising = right[i + 1] + up[i] * rising
        sums.append(rising)
        k = count - 2 - i
        falling = right[k] + down[k] * falling
    return falling * first_inv, rising * last_inv, sums


def substitute(sums, through, gaps, up, last_inv, low, high, count):
    values = [None] * count
    values[count - 1] = ((sums[count - 1] + through[count - 2] * low) - high) * last_inv
    for i in range(count - 2, -1, -1):
        inner = low if i == 0 else through[i - 1] * low
        values[i] = up[i] * (values[i + 1] + gaps[i] * (sums[i] + inner))
    return values


def local_step(sizes, sizes_mesh, pressure, source, porosity, permeability, speed):
    nx, ny, nz = sizes
    count_gx, count_gy = sizes_mesh
    far_x = count_gx // NEAR_X
    far_y = count_gy // NEAR_Y
    near_x_groups = [[z * NEAR_X + x for x in range(NEAR_X)] for z in range(far_x)]
    far_x_groups = [
        [k * NEAR_X + pick[k] * RING_X + x for k in range(far_x)] for pick in PICKS for x in range(RING_X)
    ]
    near_y_groups = [[y * NEAR_Y + c for c in range(NEAR_Y)] for y in range(far_y)]
    chip_groups = [[y + c for c in range(CORES)] for y in range(0, count_gy, CORES)]
    far_y_groups = [
        [k * NEAR_Y + pick[k] * CORES + c for k in range(far_y)] for pick in PICKS for c in range(CORES)
    ]
    cells = nx * ny
    pressure = pressure.reshape(cells, nz)
    source = source.reshape(cells, nz)
    porosity = porosity.reshape(cells, nz)
    permeability = permeability.reshape(cells, nz)
    speed = speed.reshape(cells, nz)

    def call(body, shapes, scratch, *args, name):
        return pl.pallas_call(
            body,
            out_shape=[jax.ShapeDtypeStruct(s, F32) for s in shapes],
            in_specs=[pl.BlockSpec(memory_space=pltpu.VMEM)] * len(args),
            out_specs=[pl.BlockSpec(memory_space=pltpu.VMEM)] * len(shapes),
            scratch_shapes=[pltpu.VMEM(s, F32) for s in scratch],
            compiler_params=pltpu.CompilerParams(vmem_limit_bytes=32 * 1024 * 1024),
            name=name,
        )(*args)

    def rows_y(ref, j):
        return ref[pl.ds(j, nx, stride=ny), :]

    def halves_body(
        p_hbm, source_hbm, por_hbm, perm_hbm, speed_hbm,
        half_ref, near_ref, far_ref, p_ref, source_ref, por_ref, perm_ref, speed_ref, sems,
    ):
        pairs = (
            (perm_hbm, perm_ref), (speed_hbm, speed_ref), (p_hbm, p_ref),
            (source_hbm, source_ref), (por_hbm, por_ref),
        )
        copies = [pltpu.make_async_copy(a, b, sems.at[n]) for n, (a, b) in enumerate(pairs)]
        for copy in copies:
            copy.start()
        for copy in copies[:3]:
            copy.wait()
        for i in range(nx):
            root = lax.rsqrt(plane(perm_ref, i, ny).astype(F32))
            half_ref[i * ny : (i + 1) * ny, :] = (0.5 * root) * (
                root + FORCH * plane(speed_ref, i, ny).astype(F32)
            )
        even = lax.rem(lax.axis_index("gy"), 2) == 0
        for k, ref in enumerate((half_ref, p_ref)):
            low = rows_y(ref, 0)
            high = rows_y(ref, ny - 1)
            near_ref[k] = jnp.where(even, high, low)
            far_ref[k] = jnp.where(even, low, high)
        for copy in copies[3:]:
            copy.wait()

    vmem = pl.BlockSpec(memory_space=pltpu.VMEM)
    half, near_send, far_send, pressure, source, porosity = pl.pallas_call(
        halves_body,
        out_shape=[
            jax.ShapeDtypeStruct((cells, nz), F32),
            jax.ShapeDtypeStruct((2, nx, nz), F32),
            jax.ShapeDtypeStruct((2, nx, nz), F32),
            jax.ShapeDtypeStruct((cells, nz), F32),
            jax.ShapeDtypeStruct((cells, nz), F32),
            jax.ShapeDtypeStruct((cells, nz), porosity.dtype),
        ],
        in_specs=[pl.BlockSpec(memory_space=pltpu.HBM)] * 5,
        out_specs=[vmem] * 6,
        scratch_shapes=[
            pltpu.VMEM((cells, nz), permeability.dtype),
            pltpu.VMEM((cells, nz), speed.dtype),
            pltpu.SemaphoreType.DMA((5,)),
        ],
        compiler_params=pltpu.CompilerParams(vmem_limit_bytes=16 * 1024 * 1024),
        name="halves",
    )(*(pltpu.with_memory_space_constraint(a, pltpu.HBM) for a in (pressure, source, porosity, permeability, speed)))
    far_pairs = []
    for i in range(1, count_gy - 1, 2):
        far_pairs += [(i, i + 1), (i + 1, i)]
    far_got = lax.ppermute(far_send, "gy", far_pairs)
    near_got = lax.all_gather(near_send, "gy", axis=0, axis_index_groups=chip_groups)

    def inner_body(
        p_ref, source_ref, por_ref, half_ref,
        right_ref, ratio_ref, xup_ref, xthrough_ref, xdown_ref, xends_ref,
        yup_ref, ythrough_ref, ydown_ref, yends_ref,
    ):
        lane = lax.broadcasted_iota(jnp.int32, (ny, nz), 1)
        row = lax.broadcasted_iota(jnp.int32, (ny, nz), 0)
        for i in range(nx):
            ratio_ref[i * ny : (i + 1) * ny, :] = plane(por_ref, i, ny).astype(F32) * (1.0 / STEP)

        def right_side():
            for i in range(nx):
                p = plane(p_ref, i, ny)
                h = plane(half_ref, i, ny)
                flux_z = (pltpu.roll(p, nz - 1, 1) - p) / (pltpu.roll(h, nz - 1, 1) + h)
                flux_z = jnp.where(lane == nz - 1, 0.0, flux_z)
                flux_y = (pltpu.roll(p, ny - 1, 0) - p) / (pltpu.roll(h, ny - 1, 0) + h)
                flux_y = jnp.where(row == ny - 1, 0.0, flux_y)
                lap = (flux_z - pltpu.roll(flux_z, 1, 1)) + (flux_y - pltpu.roll(flux_y, 1, 0))
                right_ref[i * ny : (i + 1) * ny, :] = (lap - plane(source_ref, i, ny)) + plane(ratio_ref, i, ny) * p
                yield None

        def keep_x(i, up, through, k, down):
            xup_ref[i] = up
            xthrough_ref[i] = through
            xdown_ref[k] = down

        def keep_y(i, up, through, k, down):
            yup_ref[i] = up
            ythrough_ref[i] = through
            ydown_ref[k] = down

        xends, yends, _ = interleave(
            elimination(lambda i: plane(ratio_ref, i, ny), lambda i: plane(half_ref, i, ny), nx, keep_x),
            elimination(lambda j: rows_y(ratio_ref, j), lambda j: rows_y(half_ref, j), ny, keep_y),
            right_side(),
        )
        for k in range(5):
            xends_ref[k] = xends[k]
            yends_ref[k] = yends[k]

    right0, ratio, xup, xthrough, xdown, xends, yup, ythrough, ydown, yends = call(
        inner_body,
        [
            (cells, nz), (cells, nz), (nx - 1, ny, nz), (nx - 1, ny, nz), (nx - 1, ny, nz), (5, ny, nz),
            (ny - 1, nx, nz), (ny - 1, nx, nz), (ny - 1, nx, nz), (5, nx, nz),
        ],
        [], pressure, source, porosity, half, name="inner",
    )

    def edges_body(
        right0_ref, p_ref, half_ref, far_ref, near_ref, xup_ref, xdown_ref, xends_ref, sums_ref, send_ref, right_ref
    ):
        place = lax.axis_index("gy")
        even = lax.rem(place, 2) == 0
        right_ref[...] = right0_ref[...]
        for j, is_end, low in ((0, place == 0, True), (ny - 1, place == count_gy - 1, False)):
            other_h, other_p = (
                jnp.where(even, far_ref[k], near_ref[0, k]) if low else jnp.where(even, near_ref[1, k], far_ref[k])
                for k in range(2)
            )
            flux = (other_p - rows_y(p_ref, j)) / (other_h + rows_y(half_ref, j))
            flux = jnp.where(is_end, 0.0, flux)
            right_ref[pl.ds(j, nx, stride=ny), :] = rows_y(right_ref, j) + flux
        right = [plane(right_ref, i, ny) for i in range(nx)]
        up = [xup_ref[i] for i in range(nx - 1)]
        down = [xdown_ref[i] for i in range(nx - 1)]
        first, last, sums = offsets(right, up, down, xends_ref[3], xends_ref[4], nx)
        for i in range(nx):
            sums_ref[i] = sums[i]
        for k, value in enumerate((xends_ref[0], xends_ref[1], xends_ref[2], first, last)):
            for target in range(NEAR_X):
                send_ref[target, k] = value

    xsums, near_x = call(
        edges_body, [(nx, ny, nz), (NEAR_X, 5, ny, nz)], [(cells, nz)],
        right0, pressure, half, far_got, near_got, xup, xdown, xends, name="edges",
    )
    near_x = lax.all_to_all(near_x, "gx", 0, 0, axis_index_groups=[[g[i] for i in NEAR_X_ORDER] for g in near_x_groups])

    def ring_body(got_ref, send_ref, tree_ref):
        pieces = [tuple(got_ref[NEAR_X_ORDER.index(n), k] for k in range(5)) for n in range(NEAR_X)]
        merged, tree = join_all(pieces)
        for k in range(5):
            for target in range(far_x):
                send_ref[target, k] = merged[k]
        for k, value in enumerate(tree_values(tree)):
            tree_ref[k] = value

    far_x_send, x_tree = call(
        ring_body, [(far_x, 5, ny, nz), (3 * (NEAR_X - 1), ny, nz)], [], near_x, name="x_ring"
    )
    far_x_got = lax.all_to_all(far_x_send, "gx", 0, 0, axis_index_groups=[[g[i] for i in FAR_X_ORDER] for g in far_x_groups])

    def along_x_body(
        got_ref, tree_ref, xsums_ref, half_ref, ratio_ref, p_ref, xup_ref, xthrough_ref, xends_ref,
        yup_ref, ydown_ref, yends_ref,
        send_ref, ysums_ref, far_faces, near_faces, solved_ref,
    ):
        place = lax.axis_index("gx")
        far = place // NEAR_X
        near = lax.rem(place, NEAR_X)
        pieces = [tuple(got_ref[FAR_X_ORDER.index(n), k] for k in range(5)) for n in range(far_x)]
        _, tree = join_all(pieces)
        fluxes = face_fluxes(tree, None, None)
        zero = jnp.zeros((ny, nz), F32)
        for k, value in enumerate(fluxes):
            far_faces[k] = zero if value is None else value
        low = far_faces[far]
        high = far_faces[far + 1]
        tree = tree_of(tree_shape(NEAR_X), [tree_ref[k] for k in range(3 * (NEAR_X - 1))])
        for k, value in enumerate(face_fluxes(tree, low, high)):
            near_faces[k] = value
        low = near_faces[near]
        high = near_faces[near + 1]
        gaps = [plane(half_ref, i, ny) + plane(half_ref, i + 1, ny) for i in range(nx - 1)]
        up = [xup_ref[i] for i in range(nx - 1)]
        through = [xthrough_ref[i] for i in range(nx - 1)]
        sums = [xsums_ref[i] for i in range(nx)]
        values = substitute(sums, through, gaps, up, xends_ref[4], low, high, nx)
        for i in range(nx):
            solved_ref[i * ny : (i + 1) * ny, :] = plane(ratio_ref, i, ny) * (values[i] - plane(p_ref, i, ny))
        yright = [rows_y(solved_ref, j) for j in range(ny)]
        up = [yup_ref[j] for j in range(ny - 1)]
        down = [ydown_ref[j] for j in range(ny - 1)]
        first, last, sums = offsets(yright, up, down, yends_ref[3], yends_ref[4], ny)
        for j in range(ny):
            ysums_ref[j] = sums[j]
        for k, value in enumerate((yends_ref[0], yends_ref[1], yends_ref[2], first, last)):
            send_ref[k] = value

    pair_send, ysums = call(
        along_x_body,
        [(5, nx, nz), (ny, nx, nz)],
        [(far_x + 1, ny, nz), (NEAR_X + 1, ny, nz), (cells, nz)],
        far_x_got, x_tree, xsums, half, ratio, pressure, xup, xthrough, xends, yup, ydown, yends,
        name="along_x",
    )
    pair_got = lax.all_gather(pair_send, "gy", axis=0, axis_index_groups=near_y_groups)

    def pair_body(got_ref, send_ref, tree_ref):
        pieces = [tuple(got_ref[n, k] for k in range(5)) for n in range(NEAR_Y)]
        merged, tree = join_all(pieces)
        for k in range(5):
            for target in range(far_y):
                send_ref[target, k] = merged[k]
        for k, value in enumerate(tree_values(tree)):
            tree_ref[k] = value

    far_y_send, y_tree = call(
        pair_body, [(far_y, 5, nx, nz), (3 * (NEAR_Y - 1), nx, nz)], [], pair_got, name="y_pair"
    )
    far_y_got = lax.all_to_all(far_y_send, "gy", 0, 0, axis_index_groups=[[g[i] for i in FAR_Y_ORDER] for g in far_y_groups])

    def updated_body(
        got_ref, tree_ref, ysums_ref, half_ref, p_ref, yup_ref, ythrough_ref, yends_ref, out_ref, far_faces, near_faces
    ):
        place = lax.axis_index("gy")
        far = place // NEAR_Y
        near = lax.rem(place, NEAR_Y)
        pieces = [tuple(got_ref[FAR_Y_ORDER.index(n), k] for k in range(5)) for n in range(far_y)]
        _, tree = join_all(pieces)
        zero = jnp.zeros((nx, nz), F32)
        for k, value in enumerate(face_fluxes(tree, None, None)):
            far_faces[k] = zero if value is None else value
        low = far_faces[far]
        high = far_faces[far + 1]
        tree = tree_of(tree_shape(NEAR_Y), [tree_ref[k] for k in range(3 * (NEAR_Y - 1))])
        for k, value in enumerate(face_fluxes(tree, low, high)):
            near_faces[k] = value
        low = near_faces[near]
        high = near_faces[near + 1]
        halves = [rows_y(half_ref, j) for j in range(ny)]
        gaps = [halves[j] + halves[j + 1] for j in range(ny - 1)]
        up = [yup_ref[j] for j in range(ny - 1)]
        through = [ythrough_ref[j] for j in range(ny - 1)]
        sums = [ysums_ref[j] for j in range(ny)]
        values = substitute(sums, through, gaps, up, yends_ref[4], low, high, ny)
        for j in range(ny):
            out_ref[pl.ds(j, nx, stride=ny), :] = rows_y(p_ref, j) + values[j]

    (updated,) = call(
        updated_body,
        [(cells, nz)],
        [(far_y + 1, nx, nz), (NEAR_Y + 1, nx, nz)],
        far_y_got, y_tree, ysums, half, pressure, yup, ythrough, yends,
        name="updated",
    )
    return updated.reshape(nx, ny, nz)


def solution(mesh):
    spec = P("gx", "gy", None)
    sizes_mesh = (mesh.shape["gx"], mesh.shape["gy"])

    def local(pressure, source, porosity, permeability, speed):
        return local_step(
            pressure.shape, sizes_mesh, pressure, source, porosity, permeability, speed
        )

    return jax.shard_map(
        local, mesh=mesh, in_specs=(spec,) * 5, out_specs=spec, check_vma=False
    )
```

```python
import jax
import jax.numpy as jnp
from jax import lax
from jax.experimental import pallas as pl
from jax.experimental.pallas import tpu as pltpu
from jax.sharding import PartitionSpec as P

FORCH = 0.55
STEP = 500.0
RING_X = 4
CORES = 2
NEAR_X = 2 * RING_X
NEAR_Y = 2 * CORES
PICKS = ((0, 1, 1, 0), (1, 0, 0, 1))
F32 = jnp.float32
NEAR_X_ORDER = (7, 6, 5, 4, 3, 2, 1, 0)
FAR_X_ORDER = (2, 3, 1, 0)
FAR_Y_ORDER = (2, 3, 1, 0)


def join(left, right):
    la, lb, lc, lg, lh = left
    ra, rb, rc, rg, rh = right
    inv = 1.0 / (lc + ra)
    left_share = lb * inv
    right_share = rb * inv
    gap = lh - rg
    merged = (
        la - lb * left_share,
        lb * right_share,
        rc - rb * right_share,
        lg - left_share * gap,
        rh + right_share * gap,
    )
    return merged, (inv * gap, left_share, right_share)


def join_all(pieces):
    if len(pieces) == 1:
        return pieces[0], None
    half = len(pieces) // 2
    left, left_tree = join_all(pieces[:half])
    right, right_tree = join_all(pieces[half:])
    merged, face = join(left, right)
    return merged, (face, left_tree, right_tree)


def face_fluxes(tree, low, high):
    if tree is None:
        return [low, high]
    face, left_tree, right_tree = tree
    flux = face[0]
    if low is not None:
        flux = flux + face[1] * low
    if high is not None:
        flux = flux + face[2] * high
    return face_fluxes(left_tree, low, flux) + face_fluxes(right_tree, flux, high)[1:]


def tree_shape(count):
    if count == 1:
        return None
    return (count, tree_shape(count // 2), tree_shape(count // 2))


def tree_values(tree):
    if tree is None:
        return []
    return list(tree[0]) + tree_values(tree[1]) + tree_values(tree[2])


def tree_of(shape, values):
    if shape is None:
        return None
    face = tuple(values.pop(0) for _ in range(3))
    left = tree_of(shape[1], values)
    return (face, left, tree_of(shape[2], values))


def plane(ref, i, rows):
    return ref[i * rows : (i + 1) * rows, :]


def elimination(ratio, half, count, keep):
    gaps = [half(i) + half(i + 1) for i in range(count - 1)]
    rising = ratio(0)
    falling = ratio(count - 1)
    through = None
    for i in range(count - 1):
        up = 1.0 / (1.0 + rising * gaps[i])
        rising = ratio(i + 1) + rising * up
        through = up if through is None else through * up
        k = count - 2 - i
        down = 1.0 / (1.0 + falling * gaps[k])
        falling = ratio(k) + falling * down
        keep(i, up, through, k, down)
        yield None
    last_inv = 1.0 / rising
    first_inv = 1.0 / falling
    yield (first_inv + half(0), through * last_inv, last_inv + half(count - 1), first_inv, last_inv)


def interleave(*parts):
    last = [None] * len(parts)
    running = list(range(len(parts)))
    while running:
        for n in list(running):
            try:
                last[n] = next(parts[n])
            except StopIteration:
                running.remove(n)
    return last


def offsets(right, up, down, first_inv, last_inv, count):
    rising = right[0]
    falling = right[count - 1]
    sums = [rising]
    for i in range(count - 1):
        rising = right[i + 1] + up[i] * rising
        sums.append(rising)
        k = count - 2 - i
        falling = right[k] + down[k] * falling
    return falling * first_inv, rising * last_inv, sums


def substitute(sums, through, gaps, up, last_inv, low, high, count):
    values = [None] * count
    values[count - 1] = ((sums[count - 1] + through[count - 2] * low) - high) * last_inv
    for i in range(count - 2, -1, -1):
        inner = low if i == 0 else through[i - 1] * low
        values[i] = up[i] * (values[i + 1] + gaps[i] * (sums[i] + inner))
    return values


def local_step(sizes, sizes_mesh, pressure, source, porosity, permeability, speed):
    nx, ny, nz = sizes
    count_gx, count_gy = sizes_mesh
    far_x = count_gx // NEAR_X
    far_y = count_gy // NEAR_Y
    near_x_groups = [[z * NEAR_X + x for x in range(NEAR_X)] for z in range(far_x)]
    far_x_groups = [
        [k * NEAR_X + pick[k] * RING_X + x for k in range(far_x)] for pick in PICKS for x in range(RING_X)
    ]
    near_y_groups = [[y * NEAR_Y + c for c in range(NEAR_Y)] for y in range(far_y)]
    chip_groups = [[y + c for c in range(CORES)] for y in range(0, count_gy, CORES)]
    far_y_groups = [
        [k * NEAR_Y + pick[k] * CORES + c for k in range(far_y)] for pick in PICKS for c in range(CORES)
    ]
    cells = nx * ny
    pressure = pressure.reshape(cells, nz)
    source = source.reshape(cells, nz)
    porosity = porosity.reshape(cells, nz)
    permeability = permeability.reshape(cells, nz)
    speed = speed.reshape(cells, nz)

    def call(body, shapes, scratch, *args, name):
        return pl.pallas_call(
            body,
            out_shape=[jax.ShapeDtypeStruct(s, F32) for s in shapes],
            in_specs=[pl.BlockSpec(memory_space=pltpu.VMEM)] * len(args),
            out_specs=[pl.BlockSpec(memory_space=pltpu.VMEM)] * len(shapes),
            scratch_shapes=[pltpu.VMEM(s, F32) for s in scratch],
            compiler_params=pltpu.CompilerParams(vmem_limit_bytes=32 * 1024 * 1024),
            name=name,
        )(*args)

    def rows_y(ref, j):
        return ref[pl.ds(j, nx, stride=ny), :]

    def halves_body(
        p_hbm, source_hbm, por_hbm, perm_hbm, speed_hbm,
        half_ref, near_ref, far_ref, p_ref, source_ref, por_ref, perm_ref, speed_ref, sems,
    ):
        pairs = (
            (perm_hbm, perm_ref), (speed_hbm, speed_ref), (p_hbm, p_ref),
            (source_hbm, source_ref), (por_hbm, por_ref),
        )
        copies = [pltpu.make_async_copy(a, b, sems.at[n]) for n, (a, b) in enumerate(pairs)]
        for copy in copies:
            copy.start()
        for copy in copies[:3]:
            copy.wait()
        for i in range(nx):
            root = lax.rsqrt(plane(perm_ref, i, ny).astype(F32))
            half_ref[i * ny : (i + 1) * ny, :] = (0.5 * root) * (
                root + FORCH * plane(speed_ref, i, ny).astype(F32)
            )
        even = lax.rem(lax.axis_index("gy"), 2) == 0
        for k, ref in enumerate((half_ref, p_ref)):
            low = rows_y(ref, 0)
            high = rows_y(ref, ny - 1)
            near_ref[k] = jnp.where(even, high, low)
            far_ref[k] = jnp.where(even, low, high)
        for copy in copies[3:]:
            copy.wait()

    vmem = pl.BlockSpec(memory_space=pltpu.VMEM)
    half, near_send, far_send, pressure, source, porosity = pl.pallas_call(
        halves_body,
        out_shape=[
            jax.ShapeDtypeStruct((cells, nz), F32),
            jax.ShapeDtypeStruct((2, nx, nz), F32),
            jax.ShapeDtypeStruct((2, nx, nz), F32),
            jax.ShapeDtypeStruct((cells, nz), F32),
            jax.ShapeDtypeStruct((cells, nz), F32),
            jax.ShapeDtypeStruct((cells, nz), porosity.dtype),
        ],
        in_specs=[pl.BlockSpec(memory_space=pltpu.HBM)] * 5,
        out_specs=[vmem] * 6,
        scratch_shapes=[
            pltpu.VMEM((cells, nz), permeability.dtype),
            pltpu.VMEM((cells, nz), speed.dtype),
            pltpu.SemaphoreType.DMA((5,)),
        ],
        compiler_params=pltpu.CompilerParams(vmem_limit_bytes=16 * 1024 * 1024),
        name="halves",
    )(*(pltpu.with_memory_space_constraint(a, pltpu.HBM) for a in (pressure, source, porosity, permeability, speed)))
    far_pairs = []
    for i in range(1, count_gy - 1, 2):
        far_pairs += [(i, i + 1), (i + 1, i)]
    far_got = lax.ppermute(far_send, "gy", far_pairs)
    near_got = lax.all_gather(near_send, "gy", axis=0, axis_index_groups=chip_groups)

    def inner_body(
        p_ref, source_ref, por_ref, half_ref,
        right_ref, ratio_ref, xup_ref, xthrough_ref, xdown_ref, xends_ref,
        yup_ref, ythrough_ref, ydown_ref, yends_ref,
    ):
        lane = lax.broadcasted_iota(jnp.int32, (ny, nz), 1)
        row = lax.broadcasted_iota(jnp.int32, (ny, nz), 0)
        for i in range(nx):
            ratio_ref[i * ny : (i + 1) * ny, :] = plane(por_ref, i, ny).astype(F32) * (1.0 / STEP)

        def right_side():
            for i in range(nx):
                p = plane(p_ref, i, ny)
                h = plane(half_ref, i, ny)
                flux_z = (pltpu.roll(p, nz - 1, 1) - p) / (pltpu.roll(h, nz - 1, 1) + h)
                flux_z = jnp.where(lane == nz - 1, 0.0, flux_z)
                flux_y = (pltpu.roll(p, ny - 1, 0) - p) / (pltpu.roll(h, ny - 1, 0) + h)
                flux_y = jnp.where(row == ny - 1, 0.0, flux_y)
                lap = (flux_z - pltpu.roll(flux_z, 1, 1)) + (flux_y - pltpu.roll(flux_y, 1, 0))
                right_ref[i * ny : (i + 1) * ny, :] = (lap - plane(source_ref, i, ny)) + plane(ratio_ref, i, ny) * p
                yield None

        def keep_x(i, up, through, k, down):
            xup_ref[i] = up
            xthrough_ref[i] = through
            xdown_ref[k] = down

        def keep_y(i, up, through, k, down):
            yup_ref[i] = up
            ythrough_ref[i] = through
            ydown_ref[k] = down

        xends, yends, _ = interleave(
            elimination(lambda i: plane(ratio_ref, i, ny), lambda i: plane(half_ref, i, ny), nx, keep_x),
            elimination(lambda j: rows_y(ratio_ref, j), lambda j: rows_y(half_ref, j), ny, keep_y),
            right_side(),
        )
        for k in range(5):
            xends_ref[k] = xends[k]
            yends_ref[k] = yends[k]

    right0, ratio, xup, xthrough, xdown, xends, yup, ythrough, ydown, yends = call(
        inner_body,
        [
            (cells, nz), (cells, nz), (nx - 1, ny, nz), (nx - 1, ny, nz), (nx - 1, ny, nz), (5, ny, nz),
            (ny - 1, nx, nz), (ny - 1, nx, nz), (ny - 1, nx, nz), (5, nx, nz),
        ],
        [], pressure, source, porosity, half, name="inner",
    )

    def edges_body(
        right0_ref, p_ref, half_ref, far_ref, near_ref, xup_ref, xdown_ref, xends_ref, sums_ref, send_ref, right_ref
    ):
        place = lax.axis_index("gy")
        even = lax.rem(place, 2) == 0
        right_ref[...] = right0_ref[...]
        for j, is_end, low in ((0, place == 0, True), (ny - 1, place == count_gy - 1, False)):
            other_h, other_p = (
                jnp.where(even, far_ref[k], near_ref[0, k]) if low else jnp.where(even, near_ref[1, k], far_ref[k])
                for k in range(2)
            )
            flux = (other_p - rows_y(p_ref, j)) / (other_h + rows_y(half_ref, j))
            flux = jnp.where(is_end, 0.0, flux)
            right_ref[pl.ds(j, nx, stride=ny), :] = rows_y(right_ref, j) + flux
        right = [plane(right_ref, i, ny) for i in range(nx)]
        up = [xup_ref[i] for i in range(nx - 1)]
        down = [xdown_ref[i] for i in range(nx - 1)]
        first, last, sums = offsets(right, up, down, xends_ref[3], xends_ref[4], nx)
        for i in range(nx):
            sums_ref[i] = sums[i]
        for k, value in enumerate((xends_ref[0], xends_ref[1], xends_ref[2], first, last)):
            for target in range(NEAR_X):
                send_ref[target, k] = value

    xsums, near_x = call(
        edges_body, [(nx, ny, nz), (NEAR_X, 5, ny, nz)], [(cells, nz)],
        right0, pressure, half, far_got, near_got, xup, xdown, xends, name="edges",
    )
    near_x = lax.all_to_all(near_x, "gx", 0, 0, axis_index_groups=[[g[i] for i in NEAR_X_ORDER] for g in near_x_groups])

    def ring_body(got_ref, send_ref, tree_ref):
        pieces = [tuple(got_ref[NEAR_X_ORDER.index(n), k] for k in range(5)) for n in range(NEAR_X)]
        merged, tree = join_all(pieces)
        for k in range(5):
            for target in range(far_x):
                send_ref[target, k] = merged[k]
        for k, value in enumerate(tree_values(tree)):
            tree_ref[k] = value

    far_x_send, x_tree = call(
        ring_body, [(far_x, 5, ny, nz), (3 * (NEAR_X - 1), ny, nz)], [], near_x, name="x_ring"
    )
    far_x_got = lax.all_to_all(far_x_send, "gx", 0, 0, axis_index_groups=[[g[i] for i in FAR_X_ORDER] for g in far_x_groups])

    def along_x_body(
        got_ref, tree_ref, xsums_ref, half_ref, ratio_ref, p_ref, xup_ref, xthrough_ref, xends_ref,
        yup_ref, ydown_ref, yends_ref,
        send_ref, ysums_ref, far_faces, near_faces, solved_ref,
    ):
        place = lax.axis_index("gx")
        far = place // NEAR_X
        near = lax.rem(place, NEAR_X)
        pieces = [tuple(got_ref[FAR_X_ORDER.index(n), k] for k in range(5)) for n in range(far_x)]
        _, tree = join_all(pieces)
        fluxes = face_fluxes(tree, None, None)
        zero = jnp.zeros((ny, nz), F32)
        for k, value in enumerate(fluxes):
            far_faces[k] = zero if value is None else value
        low = far_faces[far]
        high = far_faces[far + 1]
        tree = tree_of(tree_shape(NEAR_X), [tree_ref[k] for k in range(3 * (NEAR_X - 1))])
        for k, value in enumerate(face_fluxes(tree, low, high)):
            near_faces[k] = value
        low = near_faces[near]
        high = near_faces[near + 1]
        gaps = [plane(half_ref, i, ny) + plane(half_ref, i + 1, ny) for i in range(nx - 1)]
        up = [xup_ref[i] for i in range(nx - 1)]
        through = [xthrough_ref[i] for i in range(nx - 1)]
        sums = [xsums_ref[i] for i in range(nx)]
        values = substitute(sums, through, gaps, up, xends_ref[4], low, high, nx)
        for i in range(nx):
            solved_ref[i * ny : (i + 1) * ny, :] = plane(ratio_ref, i, ny) * (values[i] - plane(p_ref, i, ny))
        yright = [rows_y(solved_ref, j) for j in range(ny)]
        up = [yup_ref[j] for j in range(ny - 1)]
        down = [ydown_ref[j] for j in range(ny - 1)]
        first, last, sums = offsets(yright, up, down, yends_ref[3], yends_ref[4], ny)
        for j in range(ny):
            ysums_ref[j] = sums[j]
        for k, value in enumerate((yends_ref[0], yends_ref[1], yends_ref[2], first, last)):
            send_ref[k] = value

    pair_send, ysums = call(
        along_x_body,
        [(5, nx, nz), (ny, nx, nz)],
        [(far_x + 1, ny, nz), (NEAR_X + 1, ny, nz), (cells, nz)],
        far_x_got, x_tree, xsums, half, ratio, pressure, xup, xthrough, xends, yup, ydown, yends,
        name="along_x",
    )
    pair_got = lax.all_gather(pair_send, "gy", axis=0, axis_index_groups=near_y_groups)

    def pair_body(got_ref, send_ref, tree_ref):
        pieces = [tuple(got_ref[n, k] for k in range(5)) for n in range(NEAR_Y)]
        merged, tree = join_all(pieces)
        for k in range(5):
            for target in range(far_y):
                send_ref[target, k] = merged[k]
        for k, value in enumerate(tree_values(tree)):
            tree_ref[k] = value

    far_y_send, y_tree = call(
        pair_body, [(far_y, 5, nx, nz), (3 * (NEAR_Y - 1), nx, nz)], [], pair_got, name="y_pair"
    )
    far_y_got = lax.all_to_all(far_y_send, "gy", 0, 0, axis_index_groups=[[g[i] for i in FAR_Y_ORDER] for g in far_y_groups])

    def updated_body(
        got_ref, tree_ref, ysums_ref, half_ref, p_ref, yup_ref, ythrough_ref, yends_ref, out_ref, far_faces, near_faces
    ):
        place = lax.axis_index("gy")
        far = place // NEAR_Y
        near = lax.rem(place, NEAR_Y)
        pieces = [tuple(got_ref[FAR_Y_ORDER.index(n), k] for k in range(5)) for n in range(far_y)]
        _, tree = join_all(pieces)
        zero = jnp.zeros((nx, nz), F32)
        for k, value in enumerate(face_fluxes(tree, None, None)):
            far_faces[k] = zero if value is None else value
        low = far_faces[far]
        high = far_faces[far + 1]
        tree = tree_of(tree_shape(NEAR_Y), [tree_ref[k] for k in range(3 * (NEAR_Y - 1))])
        for k, value in enumerate(face_fluxes(tree, low, high)):
            near_faces[k] = value
        low = near_faces[near]
        high = near_faces[near + 1]
        halves = [rows_y(half_ref, j) for j in range(ny)]
        gaps = [halves[j] + halves[j + 1] for j in range(ny - 1)]
        up = [yup_ref[j] for j in range(ny - 1)]
        through = [ythrough_ref[j] for j in range(ny - 1)]
        sums = [ysums_ref[j] for j in range(ny)]
        values = substitute(sums, through, gaps, up, yends_ref[4], low, high, ny)
        for j in range(ny):
            out_ref[pl.ds(j, nx, stride=ny), :] = rows_y(p_ref, j) + values[j]

    (updated,) = call(
        updated_body,
        [(cells, nz)],
        [(far_y + 1, nx, nz), (NEAR_Y + 1, nx, nz)],
        far_y_got, y_tree, ysums, half, pressure, yup, ythrough, yends,
        name="updated",
    )
    return updated.reshape(nx, ny, nz)


def solution(mesh):
    spec = P("gx", "gy", None)
    sizes_mesh = (mesh.shape["gx"], mesh.shape["gy"])

    def local(pressure, source, porosity, permeability, speed):
        return local_step(
            pressure.shape, sizes_mesh, pressure, source, porosity, permeability, speed
        )

    return jax.shard_map(
        local, mesh=mesh, in_specs=(spec,) * 5, out_specs=spec, check_vma=False
    )
```

```python
import jax
import jax.numpy as jnp
from jax import lax
from jax.experimental import pallas as pl
from jax.experimental.pallas import tpu as pltpu
from jax.sharding import PartitionSpec as P

FORCH = 0.55
STEP = 500.0
RING_X = 4
CORES = 2
NEAR_X = 2 * RING_X
NEAR_Y = 2 * CORES
PICKS = ((0, 1, 1, 0), (1, 0, 0, 1))
F32 = jnp.float32
NEAR_X_ORDER = (6, 7, 5, 4, 3, 2, 1, 0)
FAR_X_ORDER = (2, 3, 1, 0)
FAR_Y_ORDER = (2, 3, 1, 0)


def join(left, right):
    la, lb, lc, lg, lh = left
    ra, rb, rc, rg, rh = right
    inv = 1.0 / (lc + ra)
    left_share = lb * inv
    right_share = rb * inv
    gap = lh - rg
    merged = (
        la - lb * left_share,
        lb * right_share,
        rc - rb * right_share,
        lg - left_share * gap,
        rh + right_share * gap,
    )
    return merged, (inv * gap, left_share, right_share)


def join_all(pieces):
    if len(pieces) == 1:
        return pieces[0], None
    half = len(pieces) // 2
    left, left_tree = join_all(pieces[:half])
    right, right_tree = join_all(pieces[half:])
    merged, face = join(left, right)
    return merged, (face, left_tree, right_tree)


def face_fluxes(tree, low, high):
    if tree is None:
        return [low, high]
    face, left_tree, right_tree = tree
    flux = face[0]
    if low is not None:
        flux = flux + face[1] * low
    if high is not None:
        flux = flux + face[2] * high
    return face_fluxes(left_tree, low, flux) + face_fluxes(right_tree, flux, high)[1:]


def tree_shape(count):
    if count == 1:
        return None
    return (count, tree_shape(count // 2), tree_shape(count // 2))


def tree_values(tree):
    if tree is None:
        return []
    return list(tree[0]) + tree_values(tree[1]) + tree_values(tree[2])


def tree_of(shape, values):
    if shape is None:
        return None
    face = tuple(values.pop(0) for _ in range(3))
    left = tree_of(shape[1], values)
    return (face, left, tree_of(shape[2], values))


def plane(ref, i, rows):
    return ref[i * rows : (i + 1) * rows, :]


def elimination(ratio, half, count, keep):
    gaps = [half(i) + half(i + 1) for i in range(count - 1)]
    rising = ratio(0)
    falling = ratio(count - 1)
    through = None
    for i in range(count - 1):
        up = 1.0 / (1.0 + rising * gaps[i])
        rising = ratio(i + 1) + rising * up
        through = up if through is None else through * up
        k = count - 2 - i
        down = 1.0 / (1.0 + falling * gaps[k])
        falling = ratio(k) + falling * down
        keep(i, up, through, k, down)
        yield None
    last_inv = 1.0 / rising
    first_inv = 1.0 / falling
    yield (first_inv + half(0), through * last_inv, last_inv + half(count - 1), first_inv, last_inv)


def interleave(*parts):
    last = [None] * len(parts)
    running = list(range(len(parts)))
    while running:
        for n in list(running):
            try:
                last[n] = next(parts[n])
            except StopIteration:
                running.remove(n)
    return last


def offsets(right, up, down, first_inv, last_inv, count):
    rising = right[0]
    falling = right[count - 1]
    sums = [rising]
    for i in range(count - 1):
        rising = right[i + 1] + up[i] * rising
        sums.append(rising)
        k = count - 2 - i
        falling = right[k] + down[k] * falling
    return falling * first_inv, rising * last_inv, sums


def substitute(sums, through, gaps, up, last_inv, low, high, count):
    values = [None] * count
    values[count - 1] = ((sums[count - 1] + through[count - 2] * low) - high) * last_inv
    for i in range(count - 2, -1, -1):
        inner = low if i == 0 else through[i - 1] * low
        values[i] = up[i] * (values[i + 1] + gaps[i] * (sums[i] + inner))
    return values


def local_step(sizes, sizes_mesh, pressure, source, porosity, permeability, speed):
    nx, ny, nz = sizes
    count_gx, count_gy = sizes_mesh
    far_x = count_gx // NEAR_X
    far_y = count_gy // NEAR_Y
    near_x_groups = [[z * NEAR_X + x for x in range(NEAR_X)] for z in range(far_x)]
    far_x_groups = [
        [k * NEAR_X + pick[k] * RING_X + x for k in range(far_x)] for pick in PICKS for x in range(RING_X)
    ]
    near_y_groups = [[y * NEAR_Y + c for c in range(NEAR_Y)] for y in range(far_y)]
    chip_groups = [[y + c for c in range(CORES)] for y in range(0, count_gy, CORES)]
    far_y_groups = [
        [k * NEAR_Y + pick[k] * CORES + c for k in range(far_y)] for pick in PICKS for c in range(CORES)
    ]
    cells = nx * ny
    pressure = pressure.reshape(cells, nz)
    source = source.reshape(cells, nz)
    porosity = porosity.reshape(cells, nz)
    permeability = permeability.reshape(cells, nz)
    speed = speed.reshape(cells, nz)

    def call(body, shapes, scratch, *args, name):
        return pl.pallas_call(
            body,
            out_shape=[jax.ShapeDtypeStruct(s, F32) for s in shapes],
            in_specs=[pl.BlockSpec(memory_space=pltpu.VMEM)] * len(args),
            out_specs=[pl.BlockSpec(memory_space=pltpu.VMEM)] * len(shapes),
            scratch_shapes=[pltpu.VMEM(s, F32) for s in scratch],
            compiler_params=pltpu.CompilerParams(vmem_limit_bytes=32 * 1024 * 1024),
            name=name,
        )(*args)

    def rows_y(ref, j):
        return ref[pl.ds(j, nx, stride=ny), :]

    def halves_body(
        p_hbm, source_hbm, por_hbm, perm_hbm, speed_hbm,
        half_ref, near_ref, far_ref, p_ref, source_ref, por_ref, perm_ref, speed_ref, sems,
    ):
        pairs = (
            (perm_hbm, perm_ref), (speed_hbm, speed_ref), (p_hbm, p_ref),
            (source_hbm, source_ref), (por_hbm, por_ref),
        )
        copies = [pltpu.make_async_copy(a, b, sems.at[n]) for n, (a, b) in enumerate(pairs)]
        for copy in copies:
            copy.start()
        for copy in copies[:3]:
            copy.wait()
        for i in range(nx):
            root = lax.rsqrt(plane(perm_ref, i, ny).astype(F32))
            half_ref[i * ny : (i + 1) * ny, :] = (0.5 * root) * (
                root + FORCH * plane(speed_ref, i, ny).astype(F32)
            )
        even = lax.rem(lax.axis_index("gy"), 2) == 0
        for k, ref in enumerate((half_ref, p_ref)):
            low = rows_y(ref, 0)
            high = rows_y(ref, ny - 1)
            near_ref[k] = jnp.where(even, high, low)
            far_ref[k] = jnp.where(even, low, high)
        for copy in copies[3:]:
            copy.wait()

    vmem = pl.BlockSpec(memory_space=pltpu.VMEM)
    half, near_send, far_send, pressure, source, porosity = pl.pallas_call(
        halves_body,
        out_shape=[
            jax.ShapeDtypeStruct((cells, nz), F32),
            jax.ShapeDtypeStruct((2, nx, nz), F32),
            jax.ShapeDtypeStruct((2, nx, nz), F32),
            jax.ShapeDtypeStruct((cells, nz), F32),
            jax.ShapeDtypeStruct((cells, nz), F32),
            jax.ShapeDtypeStruct((cells, nz), porosity.dtype),
        ],
        in_specs=[pl.BlockSpec(memory_space=pltpu.HBM)] * 5,
        out_specs=[vmem] * 6,
        scratch_shapes=[
            pltpu.VMEM((cells, nz), permeability.dtype),
            pltpu.VMEM((cells, nz), speed.dtype),
            pltpu.SemaphoreType.DMA((5,)),
        ],
        compiler_params=pltpu.CompilerParams(vmem_limit_bytes=16 * 1024 * 1024),
        name="halves",
    )(*(pltpu.with_memory_space_constraint(a, pltpu.HBM) for a in (pressure, source, porosity, permeability, speed)))
    far_pairs = []
    for i in range(1, count_gy - 1, 2):
        far_pairs += [(i, i + 1), (i + 1, i)]
    far_got = lax.ppermute(far_send, "gy", far_pairs)
    near_got = lax.all_gather(near_send, "gy", axis=0, axis_index_groups=chip_groups)

    def inner_body(
        p_ref, source_ref, por_ref, half_ref,
        right_ref, ratio_ref, xup_ref, xthrough_ref, xdown_ref, xends_ref,
        yup_ref, ythrough_ref, ydown_ref, yends_ref,
    ):
        lane = lax.broadcasted_iota(jnp.int32, (ny, nz), 1)
        row = lax.broadcasted_iota(jnp.int32, (ny, nz), 0)
        for i in range(nx):
            ratio_ref[i * ny : (i + 1) * ny, :] = plane(por_ref, i, ny).astype(F32) * (1.0 / STEP)

        def right_side():
            for i in range(nx):
                p = plane(p_ref, i, ny)
                h = plane(half_ref, i, ny)
                flux_z = (pltpu.roll(p, nz - 1, 1) - p) / (pltpu.roll(h, nz - 1, 1) + h)
                flux_z = jnp.where(lane == nz - 1, 0.0, flux_z)
                flux_y = (pltpu.roll(p, ny - 1, 0) - p) / (pltpu.roll(h, ny - 1, 0) + h)
                flux_y = jnp.where(row == ny - 1, 0.0, flux_y)
                lap = (flux_z - pltpu.roll(flux_z, 1, 1)) + (flux_y - pltpu.roll(flux_y, 1, 0))
                right_ref[i * ny : (i + 1) * ny, :] = (lap - plane(source_ref, i, ny)) + plane(ratio_ref, i, ny) * p
                yield None

        def keep_x(i, up, through, k, down):
            xup_ref[i] = up
            xthrough_ref[i] = through
            xdown_ref[k] = down

        def keep_y(i, up, through, k, down):
            yup_ref[i] = up
            ythrough_ref[i] = through
            ydown_ref[k] = down

        xends, yends, _ = interleave(
            elimination(lambda i: plane(ratio_ref, i, ny), lambda i: plane(half_ref, i, ny), nx, keep_x),
            elimination(lambda j: rows_y(ratio_ref, j), lambda j: rows_y(half_ref, j), ny, keep_y),
            right_side(),
        )
        for k in range(5):
            xends_ref[k] = xends[k]
            yends_ref[k] = yends[k]

    right0, ratio, xup, xthrough, xdown, xends, yup, ythrough, ydown, yends = call(
        inner_body,
        [
            (cells, nz), (cells, nz), (nx - 1, ny, nz), (nx - 1, ny, nz), (nx - 1, ny, nz), (5, ny, nz),
            (ny - 1, nx, nz), (ny - 1, nx, nz), (ny - 1, nx, nz), (5, nx, nz),
        ],
        [], pressure, source, porosity, half, name="inner",
    )

    def edges_body(
        right0_ref, p_ref, half_ref, far_ref, near_ref, xup_ref, xdown_ref, xends_ref, sums_ref, send_ref, right_ref
    ):
        place = lax.axis_index("gy")
        even = lax.rem(place, 2) == 0
        right_ref[...] = right0_ref[...]
        for j, is_end, low in ((0, place == 0, True), (ny - 1, place == count_gy - 1, False)):
            other_h, other_p = (
                jnp.where(even, far_ref[k], near_ref[0, k]) if low else jnp.where(even, near_ref[1, k], far_ref[k])
                for k in range(2)
            )
            flux = (other_p - rows_y(p_ref, j)) / (other_h + rows_y(half_ref, j))
            flux = jnp.where(is_end, 0.0, flux)
            right_ref[pl.ds(j, nx, stride=ny), :] = rows_y(right_ref, j) + flux
        right = [plane(right_ref, i, ny) for i in range(nx)]
        up = [xup_ref[i] for i in range(nx - 1)]
        down = [xdown_ref[i] for i in range(nx - 1)]
        first, last, sums = offsets(right, up, down, xends_ref[3], xends_ref[4], nx)
        for i in range(nx):
            sums_ref[i] = sums[i]
        for k, value in enumerate((xends_ref[0], xends_ref[1], xends_ref[2], first, last)):
            for target in range(NEAR_X):
                send_ref[target, k] = value

    xsums, near_x = call(
        edges_body, [(nx, ny, nz), (NEAR_X, 5, ny, nz)], [(cells, nz)],
        right0, pressure, half, far_got, near_got, xup, xdown, xends, name="edges",
    )
    near_x = lax.all_to_all(near_x, "gx", 0, 0, axis_index_groups=[[g[i] for i in NEAR_X_ORDER] for g in near_x_groups])

    def ring_body(got_ref, send_ref, tree_ref):
        pieces = [tuple(got_ref[NEAR_X_ORDER.index(n), k] for k in range(5)) for n in range(NEAR_X)]
        merged, tree = join_all(pieces)
        for k in range(5):
            for target in range(far_x):
                send_ref[target, k] = merged[k]
        for k, value in enumerate(tree_values(tree)):
            tree_ref[k] = value

    far_x_send, x_tree = call(
        ring_body, [(far_x, 5, ny, nz), (3 * (NEAR_X - 1), ny, nz)], [], near_x, name="x_ring"
    )
    far_x_got = lax.all_to_all(far_x_send, "gx", 0, 0, axis_index_groups=[[g[i] for i in FAR_X_ORDER] for g in far_x_groups])

    def along_x_body(
        got_ref, tree_ref, xsums_ref, half_ref, ratio_ref, p_ref, xup_ref, xthrough_ref, xends_ref,
        yup_ref, ydown_ref, yends_ref,
        send_ref, ysums_ref, far_faces, near_faces, solved_ref,
    ):
        place = lax.axis_index("gx")
        far = place // NEAR_X
        near = lax.rem(place, NEAR_X)
        pieces = [tuple(got_ref[FAR_X_ORDER.index(n), k] for k in range(5)) for n in range(far_x)]
        _, tree = join_all(pieces)
        fluxes = face_fluxes(tree, None, None)
        zero = jnp.zeros((ny, nz), F32)
        for k, value in enumerate(fluxes):
            far_faces[k] = zero if value is None else value
        low = far_faces[far]
        high = far_faces[far + 1]
        tree = tree_of(tree_shape(NEAR_X), [tree_ref[k] for k in range(3 * (NEAR_X - 1))])
        for k, value in enumerate(face_fluxes(tree, low, high)):
            near_faces[k] = value
        low = near_faces[near]
        high = near_faces[near + 1]
        gaps = [plane(half_ref, i, ny) + plane(half_ref, i + 1, ny) for i in range(nx - 1)]
        up = [xup_ref[i] for i in range(nx - 1)]
        through = [xthrough_ref[i] for i in range(nx - 1)]
        sums = [xsums_ref[i] for i in range(nx)]
        values = substitute(sums, through, gaps, up, xends_ref[4], low, high, nx)
        for i in range(nx):
            solved_ref[i * ny : (i + 1) * ny, :] = plane(ratio_ref, i, ny) * (values[i] - plane(p_ref, i, ny))
        yright = [rows_y(solved_ref, j) for j in range(ny)]
        up = [yup_ref[j] for j in range(ny - 1)]
        down = [ydown_ref[j] for j in range(ny - 1)]
        first, last, sums = offsets(yright, up, down, yends_ref[3], yends_ref[4], ny)
        for j in range(ny):
            ysums_ref[j] = sums[j]
        for k, value in enumerate((yends_ref[0], yends_ref[1], yends_ref[2], first, last)):
            send_ref[k] = value

    pair_send, ysums = call(
        along_x_body,
        [(5, nx, nz), (ny, nx, nz)],
        [(far_x + 1, ny, nz), (NEAR_X + 1, ny, nz), (cells, nz)],
        far_x_got, x_tree, xsums, half, ratio, pressure, xup, xthrough, xends, yup, ydown, yends,
        name="along_x",
    )
    pair_got = lax.all_gather(pair_send, "gy", axis=0, axis_index_groups=near_y_groups)

    def pair_body(got_ref, send_ref, tree_ref):
        pieces = [tuple(got_ref[n, k] for k in range(5)) for n in range(NEAR_Y)]
        merged, tree = join_all(pieces)
        for k in range(5):
            for target in range(far_y):
                send_ref[target, k] = merged[k]
        for k, value in enumerate(tree_values(tree)):
            tree_ref[k] = value

    far_y_send, y_tree = call(
        pair_body, [(far_y, 5, nx, nz), (3 * (NEAR_Y - 1), nx, nz)], [], pair_got, name="y_pair"
    )
    far_y_got = lax.all_to_all(far_y_send, "gy", 0, 0, axis_index_groups=[[g[i] for i in FAR_Y_ORDER] for g in far_y_groups])

    def updated_body(
        got_ref, tree_ref, ysums_ref, half_ref, p_ref, yup_ref, ythrough_ref, yends_ref, out_ref, far_faces, near_faces
    ):
        place = lax.axis_index("gy")
        far = place // NEAR_Y
        near = lax.rem(place, NEAR_Y)
        pieces = [tuple(got_ref[FAR_Y_ORDER.index(n), k] for k in range(5)) for n in range(far_y)]
        _, tree = join_all(pieces)
        zero = jnp.zeros((nx, nz), F32)
        for k, value in enumerate(face_fluxes(tree, None, None)):
            far_faces[k] = zero if value is None else value
        low = far_faces[far]
        high = far_faces[far + 1]
        tree = tree_of(tree_shape(NEAR_Y), [tree_ref[k] for k in range(3 * (NEAR_Y - 1))])
        for k, value in enumerate(face_fluxes(tree, low, high)):
            near_faces[k] = value
        low = near_faces[near]
        high = near_faces[near + 1]
        halves = [rows_y(half_ref, j) for j in range(ny)]
        gaps = [halves[j] + halves[j + 1] for j in range(ny - 1)]
        up = [yup_ref[j] for j in range(ny - 1)]
        through = [ythrough_ref[j] for j in range(ny - 1)]
        sums = [ysums_ref[j] for j in range(ny)]
        values = substitute(sums, through, gaps, up, yends_ref[4], low, high, ny)
        for j in range(ny):
            out_ref[pl.ds(j, nx, stride=ny), :] = rows_y(p_ref, j) + values[j]

    (updated,) = call(
        updated_body,
        [(cells, nz)],
        [(far_y + 1, nx, nz), (NEAR_Y + 1, nx, nz)],
        far_y_got, y_tree, ysums, half, pressure, yup, ythrough, yends,
        name="updated",
    )
    return updated.reshape(nx, ny, nz)


def solution(mesh):
    spec = P("gx", "gy", None)
    sizes_mesh = (mesh.shape["gx"], mesh.shape["gy"])

    def local(pressure, source, porosity, permeability, speed):
        return local_step(
            pressure.shape, sizes_mesh, pressure, source, porosity, permeability, speed
        )

    return jax.shard_map(
        local, mesh=mesh, in_specs=(spec,) * 5, out_specs=spec, check_vma=False
    )
```

```python
import jax
import jax.numpy as jnp
from jax import lax
from jax.experimental import pallas as pl
from jax.experimental.pallas import tpu as pltpu
from jax.sharding import PartitionSpec as P

FORCH = 0.55
STEP = 500.0
RING_X = 4
CORES = 2
NEAR_X = 2 * RING_X
NEAR_Y = 2 * CORES
PICKS = ((0, 1, 1, 0), (1, 0, 0, 1))
F32 = jnp.float32
NEAR_X_ORDER = (6, 7, 5, 4, 3, 2, 1, 0)
FAR_X_ORDER = (2, 3, 1, 0)
FAR_Y_ORDER = (2, 1, 3, 0)


def join(left, right):
    la, lb, lc, lg, lh = left
    ra, rb, rc, rg, rh = right
    inv = 1.0 / (lc + ra)
    left_share = lb * inv
    right_share = rb * inv
    gap = lh - rg
    merged = (
        la - lb * left_share,
        lb * right_share,
        rc - rb * right_share,
        lg - left_share * gap,
        rh + right_share * gap,
    )
    return merged, (inv * gap, left_share, right_share)


def join_all(pieces):
    if len(pieces) == 1:
        return pieces[0], None
    half = len(pieces) // 2
    left, left_tree = join_all(pieces[:half])
    right, right_tree = join_all(pieces[half:])
    merged, face = join(left, right)
    return merged, (face, left_tree, right_tree)


def face_fluxes(tree, low, high):
    if tree is None:
        return [low, high]
    face, left_tree, right_tree = tree
    flux = face[0]
    if low is not None:
        flux = flux + face[1] * low
    if high is not None:
        flux = flux + face[2] * high
    return face_fluxes(left_tree, low, flux) + face_fluxes(right_tree, flux, high)[1:]


def tree_shape(count):
    if count == 1:
        return None
    return (count, tree_shape(count // 2), tree_shape(count // 2))


def tree_values(tree):
    if tree is None:
        return []
    return list(tree[0]) + tree_values(tree[1]) + tree_values(tree[2])


def tree_of(shape, values):
    if shape is None:
        return None
    face = tuple(values.pop(0) for _ in range(3))
    left = tree_of(shape[1], values)
    return (face, left, tree_of(shape[2], values))


def plane(ref, i, rows):
    return ref[i * rows : (i + 1) * rows, :]


def elimination(ratio, half, count, keep):
    gaps = [half(i) + half(i + 1) for i in range(count - 1)]
    rising = ratio(0)
    falling = ratio(count - 1)
    through = None
    for i in range(count - 1):
        up = 1.0 / (1.0 + rising * gaps[i])
        rising = ratio(i + 1) + rising * up
        through = up if through is None else through * up
        k = count - 2 - i
        down = 1.0 / (1.0 + falling * gaps[k])
        falling = ratio(k) + falling * down
        keep(i, up, through, k, down)
        yield None
    last_inv = 1.0 / rising
    first_inv = 1.0 / falling
    yield (first_inv + half(0), through * last_inv, last_inv + half(count - 1), first_inv, last_inv)


def interleave(*parts):
    last = [None] * len(parts)
    running = list(range(len(parts)))
    while running:
        for n in list(running):
            try:
                last[n] = next(parts[n])
            except StopIteration:
                running.remove(n)
    return last


def offsets(right, up, down, first_inv, last_inv, count):
    rising = right[0]
    falling = right[count - 1]
    sums = [rising]
    for i in range(count - 1):
        rising = right[i + 1] + up[i] * rising
        sums.append(rising)
        k = count - 2 - i
        falling = right[k] + down[k] * falling
    return falling * first_inv, rising * last_inv, sums


def substitute(sums, through, gaps, up, last_inv, low, high, count):
    values = [None] * count
    values[count - 1] = ((sums[count - 1] + through[count - 2] * low) - high) * last_inv
    for i in range(count - 2, -1, -1):
        inner = low if i == 0 else through[i - 1] * low
        values[i] = up[i] * (values[i + 1] + gaps[i] * (sums[i] + inner))
    return values


def local_step(sizes, sizes_mesh, pressure, source, porosity, permeability, speed):
    nx, ny, nz = sizes
    count_gx, count_gy = sizes_mesh
    far_x = count_gx // NEAR_X
    far_y = count_gy // NEAR_Y
    near_x_groups = [[z * NEAR_X + x for x in range(NEAR_X)] for z in range(far_x)]
    far_x_groups = [
        [k * NEAR_X + pick[k] * RING_X + x for k in range(far_x)] for pick in PICKS for x in range(RING_X)
    ]
    near_y_groups = [[y * NEAR_Y + c for c in range(NEAR_Y)] for y in range(far_y)]
    chip_groups = [[y + c for c in range(CORES)] for y in range(0, count_gy, CORES)]
    far_y_groups = [
        [k * NEAR_Y + pick[k] * CORES + c for k in range(far_y)] for pick in PICKS for c in range(CORES)
    ]
    cells = nx * ny
    pressure = pressure.reshape(cells, nz)
    source = source.reshape(cells, nz)
    porosity = porosity.reshape(cells, nz)
    permeability = permeability.reshape(cells, nz)
    speed = speed.reshape(cells, nz)

    def call(body, shapes, scratch, *args, name):
        return pl.pallas_call(
            body,
            out_shape=[jax.ShapeDtypeStruct(s, F32) for s in shapes],
            in_specs=[pl.BlockSpec(memory_space=pltpu.VMEM)] * len(args),
            out_specs=[pl.BlockSpec(memory_space=pltpu.VMEM)] * len(shapes),
            scratch_shapes=[pltpu.VMEM(s, F32) for s in scratch],
            compiler_params=pltpu.CompilerParams(vmem_limit_bytes=32 * 1024 * 1024),
            name=name,
        )(*args)

    def rows_y(ref, j):
        return ref[pl.ds(j, nx, stride=ny), :]

    def halves_body(
        p_hbm, source_hbm, por_hbm, perm_hbm, speed_hbm,
        half_ref, near_ref, far_ref, p_ref, source_ref, por_ref, perm_ref, speed_ref, sems,
    ):
        pairs = (
            (perm_hbm, perm_ref), (speed_hbm, speed_ref), (p_hbm, p_ref),
            (source_hbm, source_ref), (por_hbm, por_ref),
        )
        copies = [pltpu.make_async_copy(a, b, sems.at[n]) for n, (a, b) in enumerate(pairs)]
        for copy in copies:
            copy.start()
        for copy in copies[:3]:
            copy.wait()
        for i in range(nx):
            root = lax.rsqrt(plane(perm_ref, i, ny).astype(F32))
            half_ref[i * ny : (i + 1) * ny, :] = (0.5 * root) * (
                root + FORCH * plane(speed_ref, i, ny).astype(F32)
            )
        even = lax.rem(lax.axis_index("gy"), 2) == 0
        for k, ref in enumerate((half_ref, p_ref)):
            low = rows_y(ref, 0)
            high = rows_y(ref, ny - 1)
            near_ref[k] = jnp.where(even, high, low)
            far_ref[k] = jnp.where(even, low, high)
        for copy in copies[3:]:
            copy.wait()

    vmem = pl.BlockSpec(memory_space=pltpu.VMEM)
    half, near_send, far_send, pressure, source, porosity = pl.pallas_call(
        halves_body,
        out_shape=[
            jax.ShapeDtypeStruct((cells, nz), F32),
            jax.ShapeDtypeStruct((2, nx, nz), F32),
            jax.ShapeDtypeStruct((2, nx, nz), F32),
            jax.ShapeDtypeStruct((cells, nz), F32),
            jax.ShapeDtypeStruct((cells, nz), F32),
            jax.ShapeDtypeStruct((cells, nz), porosity.dtype),
        ],
        in_specs=[pl.BlockSpec(memory_space=pltpu.HBM)] * 5,
        out_specs=[vmem] * 6,
        scratch_shapes=[
            pltpu.VMEM((cells, nz), permeability.dtype),
            pltpu.VMEM((cells, nz), speed.dtype),
            pltpu.SemaphoreType.DMA((5,)),
        ],
        compiler_params=pltpu.CompilerParams(vmem_limit_bytes=16 * 1024 * 1024),
        name="halves",
    )(*(pltpu.with_memory_space_constraint(a, pltpu.HBM) for a in (pressure, source, porosity, permeability, speed)))
    far_pairs = []
    for i in range(1, count_gy - 1, 2):
        far_pairs += [(i, i + 1), (i + 1, i)]
    far_got = lax.ppermute(far_send, "gy", far_pairs)
    near_got = lax.all_gather(near_send, "gy", axis=0, axis_index_groups=chip_groups)

    def inner_body(
        p_ref, source_ref, por_ref, half_ref,
        right_ref, ratio_ref, xup_ref, xthrough_ref, xdown_ref, xends_ref,
        yup_ref, ythrough_ref, ydown_ref, yends_ref,
    ):
        lane = lax.broadcasted_iota(jnp.int32, (ny, nz), 1)
        row = lax.broadcasted_iota(jnp.int32, (ny, nz), 0)
        for i in range(nx):
            ratio_ref[i * ny : (i + 1) * ny, :] = plane(por_ref, i, ny).astype(F32) * (1.0 / STEP)

        def right_side():
            for i in range(nx):
                p = plane(p_ref, i, ny)
                h = plane(half_ref, i, ny)
                flux_z = (pltpu.roll(p, nz - 1, 1) - p) / (pltpu.roll(h, nz - 1, 1) + h)
                flux_z = jnp.where(lane == nz - 1, 0.0, flux_z)
                flux_y = (pltpu.roll(p, ny - 1, 0) - p) / (pltpu.roll(h, ny - 1, 0) + h)
                flux_y = jnp.where(row == ny - 1, 0.0, flux_y)
                lap = (flux_z - pltpu.roll(flux_z, 1, 1)) + (flux_y - pltpu.roll(flux_y, 1, 0))
                right_ref[i * ny : (i + 1) * ny, :] = (lap - plane(source_ref, i, ny)) + plane(ratio_ref, i, ny) * p
                yield None

        def keep_x(i, up, through, k, down):
            xup_ref[i] = up
            xthrough_ref[i] = through
            xdown_ref[k] = down

        def keep_y(i, up, through, k, down):
            yup_ref[i] = up
            ythrough_ref[i] = through
            ydown_ref[k] = down

        xends, yends, _ = interleave(
            elimination(lambda i: plane(ratio_ref, i, ny), lambda i: plane(half_ref, i, ny), nx, keep_x),
            elimination(lambda j: rows_y(ratio_ref, j), lambda j: rows_y(half_ref, j), ny, keep_y),
            right_side(),
        )
        for k in range(5):
            xends_ref[k] = xends[k]
            yends_ref[k] = yends[k]

    right0, ratio, xup, xthrough, xdown, xends, yup, ythrough, ydown, yends = call(
        inner_body,
        [
            (cells, nz), (cells, nz), (nx - 1, ny, nz), (nx - 1, ny, nz), (nx - 1, ny, nz), (5, ny, nz),
            (ny - 1, nx, nz), (ny - 1, nx, nz), (ny - 1, nx, nz), (5, nx, nz),
        ],
        [], pressure, source, porosity, half, name="inner",
    )

    def edges_body(
        right0_ref, p_ref, half_ref, far_ref, near_ref, xup_ref, xdown_ref, xends_ref, sums_ref, send_ref, right_ref
    ):
        place = lax.axis_index("gy")
        even = lax.rem(place, 2) == 0
        right_ref[...] = right0_ref[...]
        for j, is_end, low in ((0, place == 0, True), (ny - 1, place == count_gy - 1, False)):
            other_h, other_p = (
                jnp.where(even, far_ref[k], near_ref[0, k]) if low else jnp.where(even, near_ref[1, k], far_ref[k])
                for k in range(2)
            )
            flux = (other_p - rows_y(p_ref, j)) / (other_h + rows_y(half_ref, j))
            flux = jnp.where(is_end, 0.0, flux)
            right_ref[pl.ds(j, nx, stride=ny), :] = rows_y(right_ref, j) + flux
        right = [plane(right_ref, i, ny) for i in range(nx)]
        up = [xup_ref[i] for i in range(nx - 1)]
        down = [xdown_ref[i] for i in range(nx - 1)]
        first, last, sums = offsets(right, up, down, xends_ref[3], xends_ref[4], nx)
        for i in range(nx):
            sums_ref[i] = sums[i]
        for k, value in enumerate((xends_ref[0], xends_ref[1], xends_ref[2], first, last)):
            for target in range(NEAR_X):
                send_ref[target, k] = value

    xsums, near_x = call(
        edges_body, [(nx, ny, nz), (NEAR_X, 5, ny, nz)], [(cells, nz)],
        right0, pressure, half, far_got, near_got, xup, xdown, xends, name="edges",
    )
    near_x = lax.all_to_all(near_x, "gx", 0, 0, axis_index_groups=[[g[i] for i in NEAR_X_ORDER] for g in near_x_groups])

    def ring_body(got_ref, send_ref, tree_ref):
        pieces = [tuple(got_ref[NEAR_X_ORDER.index(n), k] for k in range(5)) for n in range(NEAR_X)]
        merged, tree = join_all(pieces)
        for k in range(5):
            for target in range(far_x):
                send_ref[target, k] = merged[k]
        for k, value in enumerate(tree_values(tree)):
            tree_ref[k] = value

    far_x_send, x_tree = call(
        ring_body, [(far_x, 5, ny, nz), (3 * (NEAR_X - 1), ny, nz)], [], near_x, name="x_ring"
    )
    far_x_got = lax.all_to_all(far_x_send, "gx", 0, 0, axis_index_groups=[[g[i] for i in FAR_X_ORDER] for g in far_x_groups])

    def along_x_body(
        got_ref, tree_ref, xsums_ref, half_ref, ratio_ref, p_ref, xup_ref, xthrough_ref, xends_ref,
        yup_ref, ydown_ref, yends_ref,
        send_ref, ysums_ref, far_faces, near_faces, solved_ref,
    ):
        place = lax.axis_index("gx")
        far = place // NEAR_X
        near = lax.rem(place, NEAR_X)
        pieces = [tuple(got_ref[FAR_X_ORDER.index(n), k] for k in range(5)) for n in range(far_x)]
        _, tree = join_all(pieces)
        fluxes = face_fluxes(tree, None, None)
        zero = jnp.zeros((ny, nz), F32)
        for k, value in enumerate(fluxes):
            far_faces[k] = zero if value is None else value
        low = far_faces[far]
        high = far_faces[far + 1]
        tree = tree_of(tree_shape(NEAR_X), [tree_ref[k] for k in range(3 * (NEAR_X - 1))])
        for k, value in enumerate(face_fluxes(tree, low, high)):
            near_faces[k] = value
        low = near_faces[near]
        high = near_faces[near + 1]
        gaps = [plane(half_ref, i, ny) + plane(half_ref, i + 1, ny) for i in range(nx - 1)]
        up = [xup_ref[i] for i in range(nx - 1)]
        through = [xthrough_ref[i] for i in range(nx - 1)]
        sums = [xsums_ref[i] for i in range(nx)]
        values = substitute(sums, through, gaps, up, xends_ref[4], low, high, nx)
        for i in range(nx):
            solved_ref[i * ny : (i + 1) * ny, :] = plane(ratio_ref, i, ny) * (values[i] - plane(p_ref, i, ny))
        yright = [rows_y(solved_ref, j) for j in range(ny)]
        up = [yup_ref[j] for j in range(ny - 1)]
        down = [ydown_ref[j] for j in range(ny - 1)]
        first, last, sums = offsets(yright, up, down, yends_ref[3], yends_ref[4], ny)
        for j in range(ny):
            ysums_ref[j] = sums[j]
        for k, value in enumerate((yends_ref[0], yends_ref[1], yends_ref[2], first, last)):
            send_ref[k] = value

    pair_send, ysums = call(
        along_x_body,
        [(5, nx, nz), (ny, nx, nz)],
        [(far_x + 1, ny, nz), (NEAR_X + 1, ny, nz), (cells, nz)],
        far_x_got, x_tree, xsums, half, ratio, pressure, xup, xthrough, xends, yup, ydown, yends,
        name="along_x",
    )
    pair_got = lax.all_gather(pair_send, "gy", axis=0, axis_index_groups=near_y_groups)

    def pair_body(got_ref, send_ref, tree_ref):
        pieces = [tuple(got_ref[n, k] for k in range(5)) for n in range(NEAR_Y)]
        merged, tree = join_all(pieces)
        for k in range(5):
            for target in range(far_y):
                send_ref[target, k] = merged[k]
        for k, value in enumerate(tree_values(tree)):
            tree_ref[k] = value

    far_y_send, y_tree = call(
        pair_body, [(far_y, 5, nx, nz), (3 * (NEAR_Y - 1), nx, nz)], [], pair_got, name="y_pair"
    )
    far_y_got = lax.all_to_all(far_y_send, "gy", 0, 0, axis_index_groups=[[g[i] for i in FAR_Y_ORDER] for g in far_y_groups])

    def updated_body(
        got_ref, tree_ref, ysums_ref, half_ref, p_ref, yup_ref, ythrough_ref, yends_ref, out_ref, far_faces, near_faces
    ):
        place = lax.axis_index("gy")
        far = place // NEAR_Y
        near = lax.rem(place, NEAR_Y)
        pieces = [tuple(got_ref[FAR_Y_ORDER.index(n), k] for k in range(5)) for n in range(far_y)]
        _, tree = join_all(pieces)
        zero = jnp.zeros((nx, nz), F32)
        for k, value in enumerate(face_fluxes(tree, None, None)):
            far_faces[k] = zero if value is None else value
        low = far_faces[far]
        high = far_faces[far + 1]
        tree = tree_of(tree_shape(NEAR_Y), [tree_ref[k] for k in range(3 * (NEAR_Y - 1))])
        for k, value in enumerate(face_fluxes(tree, low, high)):
            near_faces[k] = value
        low = near_faces[near]
        high = near_faces[near + 1]
        halves = [rows_y(half_ref, j) for j in range(ny)]
        gaps = [halves[j] + halves[j + 1] for j in range(ny - 1)]
        up = [yup_ref[j] for j in range(ny - 1)]
        through = [ythrough_ref[j] for j in range(ny - 1)]
        sums = [ysums_ref[j] for j in range(ny)]
        values = substitute(sums, through, gaps, up, yends_ref[4], low, high, ny)
        for j in range(ny):
            out_ref[pl.ds(j, nx, stride=ny), :] = rows_y(p_ref, j) + values[j]

    (updated,) = call(
        updated_body,
        [(cells, nz)],
        [(far_y + 1, nx, nz), (NEAR_Y + 1, nx, nz)],
        far_y_got, y_tree, ysums, half, pressure, yup, ythrough, yends,
        name="updated",
    )
    return updated.reshape(nx, ny, nz)


def solution(mesh):
    spec = P("gx", "gy", None)
    sizes_mesh = (mesh.shape["gx"], mesh.shape["gy"])

    def local(pressure, source, porosity, permeability, speed):
        return local_step(
            pressure.shape, sizes_mesh, pressure, source, porosity, permeability, speed
        )

    return jax.shard_map(
        local, mesh=mesh, in_specs=(spec,) * 5, out_specs=spec, check_vma=False
    )
```
